256 devices in a mesh: seq: 128 (over y, x, z), dp: 2 (over core).
Axes of the slice: x: 4, y: 4, z: 8, core: 2. Of those that a mesh axis runs over, the one named last changes fastest.
Arguments:
- byte_states: bfloat16 [2, 16384, 4096], P('dp', 'seq'), may hold values from -8 to 8
- patch_starts: int32 [2, 4096], P('dp', 'seq'), may hold values from 0 to 16383, as said below
- patch_lengths: int32 [2, 4096], P('dp', 'seq'), may hold values from 1 to 7, as said below
- query_gain: float32 [4096], replicated, may hold values from 0.1 to 1.9
- key_gain: float32 [4096], replicated, may hold values from 0.1 to 1.9
- out_cotangent: bfloat16 [2, 4096, 4096], P('dp', 'seq'), may hold values from -6 to 6
Outputs:
- patch_out: bfloat16 [2, 4096, 4096], P('dp', 'seq')
- grad_bytes: float32 [2, 16384, 4096], P('dp', 'seq')
- grad_qgain: float32 [4096], replicated
- grad_kgain: float32 [4096], replicated
The draws below stay inside these ranges and needn't reach their ends.
Inputs may be any that keep to these rules, and one draw needn't show every extreme that they name: `patch_starts`: each device's bytes hold the starts of exactly 32 patches; starts rise, the first is 0, and each patch ends where the next starts (the last at the document's end), so a patch may run into the next device's bytes. patch_lengths[p] = patch_starts[p + 1] - patch_starts[p], and the document's end for the last patch.
All inputs are finite; a program needn't handle non-finite values.
Results may differ from the reference program's by a relative error of at most 0.0075.
The reference program's roundings to bfloat16 on the way (of `pooled`, `query`, `weights`, `dmixed_b` and `dscaled`) count: a program that leaves them out, or rounds other values in their place, can miss the bound.
Values may be sent and summed in bfloat16 or wider, within the bound.
A program may use at most 128 MiB of HBM per device.

```python
import jax
import jax.numpy as jnp
from jax import lax

HEAD_DIM = 128
MAXLEN = 8
HEADS = 32
D = 4096
PATCHES = 4096
BYTES = 16384
N_DP = 2


def boundary_table(key):
    jitter = jax.random.randint(key, (N_DP, PATCHES), 0, 4)
    slot = jnp.arange(PATCHES, dtype=jnp.int32)[None, :]
    jitter = jnp.where(slot == 0, 0, jnp.where(slot == 1, 3, jitter))
    starts = (4 * slot + jitter).astype(jnp.int32)
    ending = jnp.full((N_DP, 1), BYTES, jnp.int32)
    following = jnp.concatenate([starts[:, 1:], ending], 1)
    return (starts, (following - starts).astype(jnp.int32))


def draw_patch_starts(key, part):
    return boundary_table(key)[0]


def draw_patch_lengths(key, part):
    return boundary_table(key)[1]


def draw_byte_states(key, part):
    key = jax.random.fold_in(key, 5)
    base = jnp.clip(jax.random.normal(jax.random.fold_in(key, 1), (N_DP, BYTES, D), jnp.float32), -6.0, 6.0)
    return base.astype(jnp.bfloat16)


def shard_levels(stream_key, shape, split, least, high):
    def one(dim, parts):
        steps = jax.random.uniform(jax.random.fold_in(jax.random.fold_in(stream_key, 6), dim), (parts,), jnp.float32, least / len(split), high / len(split))
        return jnp.repeat(jnp.exp(steps), shape[dim] // parts).reshape((-1,) + (1,) * (len(shape) - dim - 1))

    factor_of = one(*split[0])
    for cut in split[1:]:
        factor_of = factor_of * one(*cut)
    return factor_of


def centred(rng, shape, width, most, cuts=(), held_as=jnp.bfloat16):
    gain = shard_levels(rng, shape, cuts, -0.22, 0.18) if cuts else 1.0
    entries = jax.random.normal(rng, shape, jnp.float32) * width * gain
    return jnp.minimum(jnp.maximum(entries, -most), most).astype(held_as)


def setup_inputs(seed: int = 0) -> dict:
    arg_keys = jax.random.split(jax.random.key(seed), 7)
    byte_states = draw_byte_states(jax.random.fold_in(arg_keys[6], 71), 0)
    patch_starts = draw_patch_starts(jax.random.fold_in(arg_keys[6], 71), 0)
    patch_lengths = draw_patch_lengths(jax.random.fold_in(arg_keys[6], 71), 0)
    query_gain = jnp.clip(1.0 + 0.18 * jax.random.normal(arg_keys[3], (D,), jnp.float32), 0.1, 1.9)
    key_gain = jnp.clip(1.0 + 0.18 * jax.random.normal(arg_keys[4], (D,), jnp.float32), 0.1, 1.9)
    out_cotangent = centred(arg_keys[5], (N_DP, PATCHES, D), 1.0, 6.0, ((0, 2), (1, 128)))
    return {"byte_states": byte_states, "patch_starts": patch_starts, "patch_lengths": patch_lengths, "query_gain": query_gain, "key_gain": key_gain, "out_cotangent": out_cotangent}


EPSILON = 1e-06

def pool_document(states, starts, lengths):
    width_all = states.shape[1]
    padded = jnp.concatenate([states, jnp.zeros((MAXLEN, width_all), jnp.bfloat16)], 0)
    summed = jnp.zeros((starts.shape[0], width_all), jnp.float32)
    for offset in range(MAXLEN):
        rows = padded[(starts + offset).astype(jnp.int32)].astype(jnp.float32)
        summed = summed + jnp.where((lengths > offset)[:, None], rows, 0.0)
    return (summed / lengths.astype(jnp.float32)[:, None]).astype(jnp.bfloat16)

def head_pass(items):
    pooled_h, cot_h, qgain_h, kgain_h = items
    count = pooled_h.shape[0]
    order = jnp.arange(count, dtype=jnp.int32)
    allowed = order[None, :] <= order[:, None]
    scale = HEAD_DIM ** (-0.5)
    pooled_f = pooled_h.astype(jnp.float32)
    query = (pooled_f * qgain_h).astype(jnp.bfloat16)
    keyed = (pooled_f * kgain_h).astype(jnp.bfloat16)
    scores = jnp.dot(query, keyed.T, preferred_element_type=jnp.float32) * scale
    scores = jnp.where(allowed, scores, -1e+30)
    top = lax.optimization_barrier(jnp.max(scores, -1, keepdims=True))
    expo = jnp.exp(scores - top)
    probs = expo / lax.optimization_barrier(jnp.sum(expo, -1, keepdims=True))
    weights = probs.astype(jnp.bfloat16)
    mixed = jnp.dot(weights, pooled_h, preferred_element_type=jnp.float32)
    spread = jnp.sqrt(lax.optimization_barrier(jnp.mean(mixed * mixed, -1, keepdims=True)) + EPSILON)
    result = (mixed / spread).astype(jnp.bfloat16)
    incoming = cot_h.astype(jnp.float32)
    dmixed = incoming / spread - mixed * (lax.optimization_barrier(jnp.sum(incoming * mixed, -1, keepdims=True)) / (HEAD_DIM * spread ** 3))
    dmixed_b = dmixed.astype(jnp.bfloat16)
    dprobs = jnp.dot(dmixed_b, pooled_h.T, preferred_element_type=jnp.float32)
    dscores = probs * (dprobs - lax.optimization_barrier(jnp.sum(probs * dprobs, -1, keepdims=True)))
    dscaled = (dscores * scale).astype(jnp.bfloat16)
    dquery = jnp.dot(dscaled, keyed, preferred_element_type=jnp.float32)
    dkey = jnp.dot(dscaled.T, query, preferred_element_type=jnp.float32)
    dvalue = jnp.dot(weights.T, dmixed_b, preferred_element_type=jnp.float32)
    dpooled = dquery * qgain_h + dkey * kgain_h + dvalue
    return (result, dpooled, lax.optimization_barrier(jnp.sum(dquery * pooled_f, 0)), lax.optimization_barrier(jnp.sum(dkey * pooled_f, 0)))

def split_heads(array):
    return array.reshape(PATCHES, HEADS, HEAD_DIM).transpose(1, 0, 2)

def join_heads(array):
    return array.transpose(1, 0, 2).reshape(PATCHES, D)

def reference(byte_states, patch_starts, patch_lengths, query_gain, key_gain, out_cotangent):
    outputs = []
    gradients = []
    qgain_total = jnp.zeros((D,), jnp.float32)
    kgain_total = jnp.zeros((D,), jnp.float32)
    for document in range(N_DP):
        starts = patch_starts[document]
        lengths = patch_lengths[document]
        pooled = pool_document(byte_states[document], starts, lengths)
        result, dpooled, dq_gain, dk_gain = lax.map(head_pass, (split_heads(pooled), split_heads(out_cotangent[document]), query_gain.reshape(HEADS, HEAD_DIM), key_gain.reshape(HEADS, HEAD_DIM)))
        outputs.append(join_heads(result))
        scaled = join_heads(dpooled) / lengths.astype(jnp.float32)[:, None]
        grad = jnp.zeros((BYTES + MAXLEN, D), jnp.float32)
        for offset in range(MAXLEN):
            grad = grad.at[(starts + offset).astype(jnp.int32)].add(jnp.where((lengths > offset)[:, None], scaled, 0.0))
        gradients.append(grad[:BYTES])
        qgain_total = qgain_total + dq_gain.reshape(D)
        kgain_total = kgain_total + dk_gain.reshape(D)
    return (jnp.stack(outputs), jnp.stack(gradients), qgain_total, kgain_total)
```

```python
import functools
import math

import jax
import jax.numpy as jnp
from jax import lax
from jax.experimental import pallas as pl
from jax.experimental.pallas import tpu as pltpu
from jax.sharding import PartitionSpec as P

f32 = jnp.float32
bf16 = jnp.bfloat16
HEAD_DIM = 128
HEADS = 32
PIECE = 32
BLOCK = 512
EPS = 1e-6
NT = (((1,), (1,)), ((), ()))
TN = (((0,), (0,)), ((), ()))


def place():
    seq = lax.axis_index("seq")
    core = lax.axis_index("dp")
    y = seq // 32
    return seq, core, y, (seq // 8) % 4, seq % 8


def at(seq, core):
    return {"seq": seq, "dp": core}


def low_block(y, core):
    return core + 2 * (((y + 1) // 2) % 2)


def owner(y, x, doc):
    block = 2 * y + x // 2
    high = block // 4
    low = block + high * (7 - 2 * block)
    half = low // 2
    return (doc * (3 - half) + (1 - doc) * half), low % 2, high


def source(y, core, i):
    low = low_block(y, core)
    high = i // 16
    block = low + high * (7 - 2 * low)
    return block * 16 + i % 16, y // 2, i * PIECE


def head_at(x, z, i):
    return ((x + i // 8) % 4) * 8 + (z + i % 8) % 8


MESH = pl.DeviceIdType.MESH


def signal(sem, seq, core):
    pl.semaphore_signal(sem, inc=1, device_id=at(seq, core), device_id_type=MESH)


def remote(src, dst, send, recv, seq, core):
    return pltpu.make_async_remote_copy(
        src_ref=src, dst_ref=dst, send_sem=send, recv_sem=recv,
        device_id=at(seq, core), device_id_type=MESH,
    )


def column(row, count):
    r = lax.broadcasted_iota(jnp.int32, (count, count), 0)
    c = lax.broadcasted_iota(jnp.int32, (count, count), 1)
    return jnp.sum(jnp.where(r == c, jnp.broadcast_to(row, (count, count)), 0), 1, keepdims=True)


def dispatch(bytes_ref, starts, lengths, cot, kfull, cot_h, pooled, sums, spill, spill_in,
             s_spill, r_spill, s_pool, r_pool, s_cot, r_cot, s_key, r_key):
    seq, core, y, x, z = place()
    oy, ocore, ohigh = owner(y, x, core)
    mine = (oy == y) & (ocore == core)
    low = low_block(y, core)
    partner = seq + 32 - 64 * (y % 2)
    before = (seq + 127) % 128
    after = (seq + 1) % 128

    barrier = pltpu.get_barrier_semaphore()

    def greet(i, _):
        s, d, _row = source(y, core, i)

        @pl.when((s != seq) | (d != core))
        def _():
            signal(barrier, s, d)

        return 0

    lax.fori_loop(0, 32, greet, 0)
    signal(barrier, seq, 1 - core)
    signal(barrier, partner, core)
    signal(barrier, after, core)

    base = seq * 128
    start = column(starts[...], PIECE) - base
    length = column(lengths[...], PIECE)
    at_byte = lax.broadcasted_iota(jnp.int32, (PIECE, 128), 1)
    member = ((at_byte >= start) & (at_byte < start + length)).astype(f32).astype(bf16)
    first = starts[:, 0:1] - base
    lead = (lax.broadcasted_iota(jnp.int32, (16, 128), 1) < first).astype(f32).astype(bf16)
    spill[...] = jnp.dot(lead, bytes_ref[...], preferred_element_type=f32)[0:1, :]

    @pl.when(mine)
    def _():
        pl.semaphore_wait(barrier, 34)

    @pl.when(jnp.logical_not(mine))
    def _():
        pl.semaphore_wait(barrier, 35)

    spilling = remote(spill, spill_in, s_spill, r_spill, before, core)
    spilling.start()
    sums[...] = jnp.dot(member, bytes_ref[...], preferred_element_type=f32)
    inverse = 1.0 / length.astype(f32)
    spilling.wait_recv()
    last = (lax.broadcasted_iota(jnp.int32, (PIECE, 1), 0) == PIECE - 1) & (seq < 127)
    pooled[...] = ((sums[...] + jnp.where(last, spill_in[...], 0.0)) * inverse).astype(bf16)

    krow = pl.multiple_of(seq * PIECE, PIECE)
    crow = pl.multiple_of(ohigh * BLOCK + (seq % 16) * PIECE, PIECE)

    def scatter(src, dst, row, send, recv):
        def step(i, _):
            h = head_at(x, z, i)
            part = src.at[:, pl.ds(pl.multiple_of(h * HEAD_DIM, HEAD_DIM), HEAD_DIM)]
            there = dst.at[pl.ds(row, PIECE), :]
            target = oy * 32 + h
            local = (target == seq) & (ocore == core)

            @pl.when(local)
            def _():
                pltpu.make_async_copy(part, there, recv).start()

            @pl.when(jnp.logical_not(local))
            def _():
                remote(part, there, send, recv, target, ocore).start()

            return 0

        lax.fori_loop(0, 32, step, 0)

    scatter(pooled, kfull, krow, s_pool, r_pool)
    scatter(cot, cot_h, crow, s_cot, r_cot)

    def rows(block):
        return kfull.at[pl.ds(pl.multiple_of(block * BLOCK, BLOCK), BLOCK), :]

    pltpu.make_async_copy(kfull.at[pl.ds(0, 1024), :], kfull.at[pl.ds(0, 1024), :], r_pool).wait()
    copies = []
    for i, block in enumerate((low, 7 - low)):
        a = remote(rows(block), rows(block), s_key.at[i], r_key.at[i], partner, core)
        b = remote(rows(block), rows(block), s_key.at[2 + i], r_key.at[2 + i], seq, 1 - core)
        a.start()
        b.start()
        copies.append((a, b))
    far = low + 2 - 4 * (low // 2)
    for i, block in enumerate((far, 7 - far)):
        copies[i][0].wait_recv()
        c = remote(rows(block), rows(block), s_key.at[4 + i], r_key.at[4 + i], seq, 1 - core)
        c.start()
        copies[i] = copies[i] + (c,)
    for a, b, c in copies:
        b.wait_recv()
        c.wait_recv()
        a.wait_send()
        b.wait_send()
        c.wait_send()
    pltpu.make_async_copy(cot_h, cot_h, r_cot).wait()
    spilling.wait_send()

    @pl.when(mine)
    def _():
        for src, sem in ((pooled, s_pool), (cot, s_cot)):
            part = src.at[:, pl.ds(0, 31 * HEAD_DIM)]
            pltpu.make_async_copy(part, part, sem).wait()

    @pl.when(jnp.logical_not(mine))
    def _():
        for src, sem in ((pooled, s_pool), (cot, s_cot)):
            pltpu.make_async_copy(src, src, sem).wait()


def give_back(starts, lengths, out_h, side, gains, patch_out, grad, gq, gk,
              to_sib, from_sib, to_far, from_far, mine_b, dpool, spill, spill_in, column_in, plane,
              s_out, r_out, s_sib, r_sib, s_far, r_far, s_dp, r_dp, s_col, r_col, s_pla, r_pla,
              s_spill, r_spill):
    seq, core, y, x, z = place()
    oy, ocore, ohigh = owner(y, x, core)
    mine = (oy == y) & (ocore == core)
    low = low_block(y, core)
    partner = seq + 32 - 64 * (y % 2)
    before = (seq + 127) % 128
    after = (seq + 1) % 128
    head = x * 8 + z

    barrier = pltpu.get_barrier_semaphore()

    def greet(i, _):
        h = head_at(x, z, i)
        target = oy * 32 + h

        @pl.when((target != seq) | (ocore != core))
        def _():
            signal(barrier, target, ocore)

        return 0

    lax.fori_loop(0, 32, greet, 0)

    def greet_plane(i, _):
        signal(barrier, y * 32 + head_at(x, z, i), core)
        return 0

    lax.fori_loop(1, 32, greet_plane, 0)

    def greet_column(i, _):
        c = (y * 2 + core + i) % 8
        signal(barrier, (c // 2) * 32 + head, c % 2)
        return 0

    lax.fori_loop(1, 8, greet_column, 0)
    signal(barrier, seq, 1 - core)
    signal(barrier, partner, core)
    signal(barrier, before, core)

    def rows(block):
        return pl.ds(pl.multiple_of(block * BLOCK, BLOCK), BLOCK)

    sib = low + 1 - 2 * (low % 2)
    far = low + 2 - 4 * (low // 2)
    farsib = sib + 2 - 4 * (sib // 2)
    for i, block in enumerate((farsib, 7 - farsib, sib, 7 - sib)):
        to_sib[i * BLOCK:(i + 1) * BLOCK, :] = side[rows(block), :].astype(bf16)
    column_in[pl.ds(y * 2 + core, 1)] = gains[...][None]

    @pl.when(mine)
    def _():
        pl.semaphore_wait(barrier, 31 + 31 + 7 + 3)

    @pl.when(jnp.logical_not(mine))
    def _():
        pl.semaphore_wait(barrier, 32 + 31 + 7 + 3)

    sib_a = remote(to_sib.at[0:1024], from_sib.at[0:1024], s_sib.at[0], r_sib.at[0], seq, 1 - core)
    sib_b = remote(to_sib.at[1024:2048], from_sib.at[1024:2048], s_sib.at[1], r_sib.at[1], seq, 1 - core)
    sib_a.start()
    sib_b.start()

    def send_column(i, _):
        c = (y * 2 + core + i) % 8
        slot = column_in.at[pl.ds(y * 2 + core, 1)]
        remote(slot, slot, s_col, r_col, (c // 2) * 32 + head, c % 2).start()
        return 0

    lax.fori_loop(1, 8, send_column, 0)

    column_of = pl.ds(pl.multiple_of(head * HEAD_DIM, HEAD_DIM), HEAD_DIM)

    def scatter(src, dst, send, recv):
        def step(i, _):
            j = (i + head) % 32
            s, d, row = source(y, core, j)
            part = src.at[pl.ds(pl.multiple_of(row, PIECE), PIECE), :]
            there = dst.at[:, column_of]
            local = (s == seq) & (d == core)

            @pl.when(local)
            def _():
                pltpu.make_async_copy(part, there, recv).start()

            @pl.when(jnp.logical_not(local))
            def _():
                remote(part, there, send, recv, s, d).start()

            return 0

        lax.fori_loop(0, 32, step, 0)

    sib_a.wait_recv()
    for i, block in enumerate((far, 7 - far)):
        half = pl.ds(i * BLOCK, BLOCK)
        to_far[half, :] = (side[rows(block), :] + from_sib[half, :].astype(f32)).astype(bf16)
    across = remote(to_far, from_far, s_far, r_far, partner, core)
    across.start()
    scatter(out_h, patch_out, s_out, r_out)

    pltpu.make_async_copy(column_in.at[0:7], column_in.at[0:7], r_col).wait()
    total = column_in[0]
    for i in range(1, 8):
        total = total + column_in[i]
    plane[pl.ds(head, 1)] = total[None]

    def send_plane(i, _):
        slot = plane.at[pl.ds(head, 1)]
        remote(slot, slot, s_pla, r_pla, y * 32 + head_at(x, z, i), core).start()
        return 0

    lax.fori_loop(1, 32, send_plane, 0)

    sib_b.wait_recv()
    across.wait_recv()
    for i, block in enumerate((low, 7 - low)):
        half = pl.ds(i * BLOCK, BLOCK)
        mine_b[half, :] = (
            side[rows(block), :]
            + from_sib[1024 + i * BLOCK:1024 + (i + 1) * BLOCK, :].astype(f32)
            + from_far[half, :].astype(f32)
        ).astype(bf16)
    scatter(mine_b, dpool, s_dp, r_dp)

    base = seq * 128
    start = starts[...] - base
    length = lengths[...]
    at_byte = lax.broadcasted_iota(jnp.int32, (128, PIECE), 0)
    inside = (at_byte >= start) & (at_byte < start + length)
    member = inside.astype(f32).astype(bf16)
    inverse = 1.0 / length.astype(f32)
    by_byte = jnp.sum(jnp.where(inside, inverse, 0.0), 1, keepdims=True)
    lead = lax.broadcasted_iota(jnp.int32, (128, 1), 0) < start[:, 0:1]

    pltpu.make_async_copy(plane.at[0:31], plane.at[0:31], r_pla).wait()
    for i in range(HEADS):
        gq[i:i + 1, :] = plane[i, 0:1, :]
        gk[i:i + 1, :] = plane[i, 1:2, :]

    pltpu.make_async_copy(dpool, dpool, r_dp).wait()
    spill[...] = dpool[16:32, :].astype(f32)[15:16, :] * inverse[:, PIECE - 1:PIECE]
    spilling = remote(spill, spill_in, s_spill, r_spill, after, core)
    spilling.start()
    grad[...] = jnp.dot(member, dpool[...], preferred_element_type=f32) * by_byte
    spilling.wait_recv()
    grad[0:8, :] = jnp.where(lead[0:8, :], spill_in[...], grad[0:8, :])

    pltpu.make_async_copy(patch_out, patch_out, r_out).wait()
    spilling.wait_send()
    sib_a.wait_send()
    sib_b.wait_send()
    across.wait_send()
    pltpu.make_async_copy(column_in.at[0:7], column_in.at[0:7], s_col).wait()
    pltpu.make_async_copy(plane.at[0:31], plane.at[0:31], s_pla).wait()

    @pl.when(mine)
    def _():
        for src, sem in ((out_h, s_out), (mine_b, s_dp)):
            part = src.at[0:31 * PIECE]
            pltpu.make_async_copy(part, part, sem).wait()

    @pl.when(jnp.logical_not(mine))
    def _():
        for src, sem in ((out_h, s_out), (mine_b, s_dp)):
            pltpu.make_async_copy(src, src, sem).wait()


SCALE=HEAD_DIM**-0.5
C2=SCALE*math.log2(math.e)

def lanes(x, op):
    acc = x[:, :128]
    for i in range(1, x.shape[1]//128):
        acc = op(acc, x[:, i*128:(i+1)*128])
    return acc

def attend(blk, first, kfull, keyed, cot, cot_row, out, s_ref, w_ref, d_ref, dk, dv, dq_ref, qgain):
    row0 = pl.multiple_of(blk * BLOCK, BLOCK)
    q = (kfull[pl.ds(row0, BLOCK), :].astype(f32) * qgain).astype(bf16)
    def rows(j): return pl.ds(pl.multiple_of(j * BLOCK, BLOCK), BLOCK)
    def scores(j, m, diag):
        s = lax.dot_general(q, keyed[rows(j), :], NT, preferred_element_type=f32)
        if diag:
            r = lax.broadcasted_iota(jnp.int32, s.shape, 0); c = lax.broadcasted_iota(jnp.int32, s.shape, 1)
            s = jnp.where(c <= r, s, -1e30)
        s_ref[:, rows(j)] = s
        return jnp.maximum(m, lanes(s, jnp.maximum))
    m = lax.fori_loop(0, blk, lambda j, m: scores(j, m, False), jnp.full((BLOCK, 128), -1e30, f32))
    m = scores(blk, m, True)
    top = jnp.max(m, -1, keepdims=True)
    def expo(j, l):
        e = jnp.exp2((s_ref[:, rows(j)] - top) * C2)
        s_ref[:, rows(j)] = e
        return l + lanes(e, jnp.add)
    l = lax.fori_loop(0, blk + 1, expo, jnp.zeros((BLOCK, 128), f32))
    inv = 1.0 / jnp.sum(l, -1, keepdims=True)
    def mix(j, acc):
        w = (s_ref[:, rows(j)] * inv).astype(bf16)
        w_ref[:, rows(j)] = w
        return acc + jnp.dot(w, kfull[rows(j), :], preferred_element_type=f32)
    mixed = lax.fori_loop(0, blk + 1, mix, jnp.zeros((BLOCK, 128), f32))
    spread = jnp.sqrt(jnp.mean(mixed * mixed, -1, keepdims=True) + EPS)
    rs = 1.0 / spread
    out[cot_row:cot_row+BLOCK, :] = (mixed * rs).astype(bf16)
    g = cot[cot_row:cot_row+BLOCK, :].astype(f32)
    dm = g * rs - mixed * (jnp.sum(g * mixed, -1, keepdims=True) * (rs * rs * rs) * (1.0 / HEAD_DIM))
    dmb = dm.astype(bf16)
    def dprob(j, r):
        dp = lax.dot_general(dmb, kfull[rows(j), :], NT, preferred_element_type=f32)
        d_ref[:, rows(j)] = dp
        v = lax.dot_general(w_ref[:, rows(j)], dmb, TN, preferred_element_type=f32)
        if first: dv[rows(j), :] = v
        else: dv[rows(j), :] += v
        return r + lanes(dp * s_ref[:, rows(j)], jnp.add)
    r = lax.fori_loop(0, blk + 1, dprob, jnp.zeros((BLOCK, 128), f32))
    r = jnp.sum(r, -1, keepdims=True) * inv
    invs = inv * SCALE
    def back(j, acc):
        ds = ((s_ref[:, rows(j)] * invs) * (d_ref[:, rows(j)] - r)).astype(bf16)
        k = lax.dot_general(ds, q, TN, preferred_element_type=f32)
        if first: dk[rows(j), :] = k
        else: dk[rows(j), :] += k
        return acc + jnp.dot(ds, keyed[rows(j), :], preferred_element_type=f32)
    dq_ref[...] = lax.fori_loop(0, blk + 1, back, jnp.zeros((BLOCK, 128), f32))

def attn_body(lo, kfull, cot, qgain, kgain, out, side, gains, keyed, s_ref, w_ref, d_ref, dk, dv, dq_ref):
    hi = 7 - lo
    def chunk(j): return pl.ds(pl.multiple_of(j * BLOCK, BLOCK), BLOCK)
    def prep(j, _):
        keyed[chunk(j), :] = (kfull[chunk(j), :].astype(f32) * kgain).astype(bf16)
        return 0
    lax.fori_loop(0, hi + 1, prep, 0)
    def clear(j, _):
        dk[chunk(j), :] = jnp.zeros((BLOCK, 128), f32)
        dv[chunk(j), :] = jnp.zeros((BLOCK, 128), f32)
        return 0
    lax.fori_loop(hi + 1, 8, clear, 0)
    attend(hi, True, kfull, keyed, cot, BLOCK, out, s_ref, w_ref, d_ref, dk, dv, dq_ref.at[1], qgain)
    attend(lo, False, kfull, keyed, cot, 0, out, s_ref, w_ref, d_ref, dk, dv, dq_ref.at[0], qgain)
    def finish(j, acc):
        d = dk[chunk(j), :]
        side[chunk(j), :] = d * kgain + dv[chunk(j), :]
        return acc + jnp.sum(d * kfull[chunk(j), :].astype(f32), 0, keepdims=True)
    gk = lax.fori_loop(0, 8, finish, jnp.zeros((1, 128), f32))
    gq = jnp.zeros((1, 128), f32)
    for i, b in ((0, lo), (1, hi)):
        dq = dq_ref[i]
        side[chunk(b), :] += dq * qgain
        gq = gq + jnp.sum(dq * kfull[chunk(b), :].astype(f32), 0, keepdims=True)
    gains[0:1, :] = gq
    gains[1:2, :] = gk


def attn_scratch():
    return [pltpu.VMEM((4096, HEAD_DIM), bf16), pltpu.VMEM((BLOCK, 4096), f32), pltpu.VMEM((BLOCK, 4096), bf16),
            pltpu.VMEM((BLOCK, 4096), f32), pltpu.VMEM((4096, HEAD_DIM), f32), pltpu.VMEM((4096, HEAD_DIM), f32),
            pltpu.VMEM((2, BLOCK, HEAD_DIM), f32)]


VMEM = pl.BlockSpec(memory_space=pltpu.VMEM)
DMA = pltpu.SemaphoreType.DMA


def shape(dims, dtype):
    return jax.ShapeDtypeStruct(dims, dtype)


def attend_kernel(kfull, cot, qgain, kgain, out, side, gains, *scratch):
    seq, core, y, x, z = place()
    head = x * 8 + z
    attn_body(low_block(y, core), kfull, cot, qgain[pl.ds(head, 1), :], kgain[pl.ds(head, 1), :],
              out, side, gains, *scratch)


def on_device(byte_states, patch_starts, patch_lengths, query_gain, key_gain, out_cotangent):
    states = byte_states[0]
    cot = out_cotangent[0]
    width = states.shape[1]
    kfull, cot_h = pl.pallas_call(
        dispatch,
        out_shape=(shape((4096, HEAD_DIM), bf16), shape((1024, HEAD_DIM), bf16)),
        in_specs=[VMEM] * 4,
        out_specs=(VMEM, VMEM),
        scratch_shapes=[
            pltpu.VMEM((PIECE, width), bf16),
            pltpu.VMEM((PIECE, width), f32),
            pltpu.VMEM((1, width), f32),
            pltpu.VMEM((1, width), f32),
            DMA, DMA, DMA, DMA, DMA, DMA, DMA((6,)), DMA((6,)),
        ],
        compiler_params=pltpu.CompilerParams(
            collective_id=0, has_side_effects=True, vmem_limit_bytes=40 << 20
        ),
    )(states, patch_starts, patch_lengths, cot)
    out_h, side, gains = pl.pallas_call(
        attend_kernel,
        out_shape=(shape((1024, HEAD_DIM), bf16), shape((4096, HEAD_DIM), f32), shape((2, HEAD_DIM), f32)),
        in_specs=[VMEM] * 4,
        out_specs=(VMEM,) * 3,
        scratch_shapes=attn_scratch(),
        compiler_params=pltpu.CompilerParams(vmem_limit_bytes=56 << 20),
    )(kfull, cot_h, query_gain.reshape(HEADS, HEAD_DIM), key_gain.reshape(HEADS, HEAD_DIM))
    patch_out, grad, gq, gk = pl.pallas_call(
        give_back,
        out_shape=(shape((PIECE, width), bf16), shape((128, width), f32),
                   shape((HEADS, HEAD_DIM), f32), shape((HEADS, HEAD_DIM), f32)),
        in_specs=[VMEM] * 5,
        out_specs=(VMEM,) * 4,
        scratch_shapes=[
            pltpu.VMEM((2048, HEAD_DIM), bf16),
            pltpu.VMEM((2048, HEAD_DIM), bf16),
            pltpu.VMEM((1024, HEAD_DIM), bf16),
            pltpu.VMEM((1024, HEAD_DIM), bf16),
            pltpu.VMEM((1024, HEAD_DIM), bf16),
            pltpu.VMEM((PIECE, width), bf16),
            pltpu.VMEM((1, width), f32),
            pltpu.VMEM((1, width), f32),
            pltpu.VMEM((8, 2, HEAD_DIM), f32),
            pltpu.VMEM((HEADS, 2, HEAD_DIM), f32),
            DMA, DMA, DMA((2,)), DMA((2,)), DMA, DMA, DMA, DMA, DMA, DMA, DMA, DMA, DMA, DMA,
        ],
        compiler_params=pltpu.CompilerParams(
            collective_id=1, has_side_effects=True, vmem_limit_bytes=48 << 20
        ),
    )(patch_starts, patch_lengths, out_h, side, gains)
    return patch_out[None], grad[None], gq.reshape(width), gk.reshape(width)


def solution(mesh):
    rows = P("dp", "seq", None)
    flat = P("dp", "seq")
    return jax.shard_map(
        on_device,
        mesh=mesh,
        in_specs=(rows, flat, flat, P(), P(), rows),
        out_specs=(rows, rows, P(), P()),
        check_vma=False,
    )
```

```python
import functools
import math

import jax
import jax.numpy as jnp
from jax import lax
from jax.experimental import pallas as pl
from jax.experimental.pallas import tpu as pltpu
from jax.sharding import PartitionSpec as P

f32 = jnp.float32
bf16 = jnp.bfloat16
HEAD_DIM = 128
HEADS = 32
PIECE = 32
BLOCK = 512
EPS = 1e-6
NT = (((1,), (1,)), ((), ()))
TN = (((0,), (0,)), ((), ()))


def place():
    seq = lax.axis_index("seq")
    core = lax.axis_index("dp")
    y = seq // 32
    return seq, core, y, (seq // 8) % 4, seq % 8


def at(seq, core):
    return {"seq": seq, "dp": core}


def low_block(y, core):
    return core + 2 * (((y + 1) // 2) % 2)


def owner(y, x, doc):
    block = 2 * y + x // 2
    high = block // 4
    low = block + high * (7 - 2 * block)
    half = low // 2
    return (doc * (3 - half) + (1 - doc) * half), low % 2, high


def source(y, core, i):
    low = low_block(y, core)
    high = i // 16
    block = low + high * (7 - 2 * low)
    return block * 16 + i % 16, y // 2, i * PIECE


def head_at(x, z, i):
    return ((x + i // 8) % 4) * 8 + (z + i % 8) % 8


MESH = pl.DeviceIdType.MESH


def signal(sem, seq, core):
    pl.semaphore_signal(sem, inc=1, device_id=at(seq, core), device_id_type=MESH)


def remote(src, dst, send, recv, seq, core):
    return pltpu.make_async_remote_copy(
        src_ref=src, dst_ref=dst, send_sem=send, recv_sem=recv,
        device_id=at(seq, core), device_id_type=MESH,
    )


def column(row, count):
    r = lax.broadcasted_iota(jnp.int32, (count, count), 0)
    c = lax.broadcasted_iota(jnp.int32, (count, count), 1)
    return jnp.sum(jnp.where(r == c, jnp.broadcast_to(row, (count, count)), 0), 1, keepdims=True)


SCALE = HEAD_DIM ** -0.5
C2 = SCALE * math.log2(math.e)
STEPS = 9
GROUP = BLOCK // HEAD_DIM


def chunk(j):
    return pl.ds(pl.multiple_of(j * BLOCK, BLOCK), BLOCK)


def lanes(x, op):
    parts = [x[:, g * HEAD_DIM:(g + 1) * HEAD_DIM] for g in range(x.shape[1] // HEAD_DIM)]
    return functools.reduce(op, parts)


def step_at(low, t):
    if isinstance(t, int):
        return {0: (0, low), 7: (1, low), 8: (1, 7 - low)}[t]
    high = (t - low + 7) // 8
    place = t - low - 1
    return high, high * (place + (place - low + 8) // 8) + (1 - high) * (low - t)


def over_steps(body, waits=None):
    body((0, 8, 7))
    if waits is not None:
        waits()

    def three(i, _):
        body(tuple(1 + 3 * i + u for u in range(3)))
        return 0

    lax.fori_loop(0, 2, three, 0)


def tiled(x):
    return jnp.concatenate([x] * GROUP, 1)


def forward(low, kfull, keyed, query, s_ref, w_ref, stat, mixed, waits=None):
    stat[...] = jnp.full(stat.shape, -1e30, f32)

    def cols(t):
        return pl.ds(pl.multiple_of(t * BLOCK, BLOCK), BLOCK)

    def scores(steps):
        for t in steps:
            high, j = step_at(low, t)
            s = lax.dot_general(query[chunk(high), :], keyed[chunk(j), :], NT, preferred_element_type=f32)
            if isinstance(t, int) and t != 7:
                r = lax.broadcasted_iota(jnp.int32, s.shape, 0)
                c = lax.broadcasted_iota(jnp.int32, s.shape, 1)
                s = jnp.where(c <= r, s, -1e30)
            s_ref[:, cols(t)] = s
            stat[chunk(high), :] = jnp.maximum(stat[chunk(high), :], lanes(s, jnp.maximum))

    over_steps(scores, waits)
    stat[...] = jnp.broadcast_to(jnp.max(stat[...], -1, keepdims=True), stat.shape)
    mixed[...] = jnp.zeros(mixed.shape, f32)

    def expo(steps):
        for t in steps:
            high, j = step_at(low, t)
            e = jnp.exp2((s_ref[:, cols(t)] - tiled(stat[chunk(high), :])) * C2)
            s_ref[:, cols(t)] = e
            mixed[chunk(high), :] += lanes(e, jnp.add)

    over_steps(expo)
    stat[...] = jnp.broadcast_to(1.0 / jnp.sum(mixed[...], -1, keepdims=True), stat.shape)
    mixed[...] = jnp.zeros(mixed.shape, f32)

    def mix(steps):
        for t in steps:
            high, j = step_at(low, t)
            w = (s_ref[:, cols(t)] * tiled(stat[chunk(high), :])).astype(bf16)
            w_ref[:, cols(t)] = w
            mixed[chunk(high), :] += jnp.dot(w, kfull[chunk(j), :], preferred_element_type=f32)

    over_steps(mix)


def normed(mixed, out):
    m = mixed[...]
    rs = 1.0 / jnp.sqrt(jnp.mean(m * m, -1, keepdims=True) + EPS)
    out[...] = (m * rs).astype(bf16)
    return rs


def backward(low, kfull, keyed, query, dmb, s_ref, w_ref, d_ref, stat, delta, dk, dv, dq):
    def cols(t):
        return pl.ds(pl.multiple_of(t * BLOCK, BLOCK), BLOCK)

    delta[...] = jnp.zeros(delta.shape, f32)

    def dprobs(steps):
        for t in steps:
            high, j = step_at(low, t)
            dp = lax.dot_general(dmb[chunk(high), :], kfull[chunk(j), :], NT, preferred_element_type=f32)
            d_ref[:, cols(t)] = dp
            dv[chunk(j), :] += lax.dot_general(w_ref[:, cols(t)], dmb[chunk(high), :], TN, preferred_element_type=f32)
            delta[chunk(high), :] += lanes(dp * s_ref[:, cols(t)], jnp.add)

    over_steps(dprobs)
    delta[...] = jnp.broadcast_to(jnp.sum(delta[...], -1, keepdims=True), delta.shape) * stat[...]
    stat[...] = stat[...] * SCALE
    dq[...] = jnp.zeros(dq.shape, f32)

    def back(steps):
        for t in steps:
            high, j = step_at(low, t)
            ds = ((s_ref[:, cols(t)] * tiled(stat[chunk(high), :]))
                  * (d_ref[:, cols(t)] - tiled(delta[chunk(high), :]))).astype(bf16)
            dk[chunk(j), :] += lax.dot_general(ds, query[chunk(high), :], TN, preferred_element_type=f32)
            dq[chunk(high), :] += jnp.dot(ds, keyed[chunk(j), :], preferred_element_type=f32)

    over_steps(back)


def whole(states, starts, lengths, qgain_all, kgain_all, cot_rows,
          patch_out, dpool, spill_back, plane,
          bytes_in, cot, pooled, sums, spill, spill_in, back, kfull, cot_h, out_h,
          keyed, query, s_ref, w_ref, d_ref, dk, dv, dq, stat, delta, mixed, dmb,
          from_sib, to_far, from_far, mine_b, column_in,
          s_load, s_spill, r_spill, s_pool, r_pool, s_cot, r_cot, s_key, r_key,
          s_out, r_out, s_sib, r_sib, s_far, r_far, s_dp, r_dp, s_col, r_col, s_pla, r_pla,
          s_back, r_back):
    seq, core, y, x, z = place()
    oy, ocore, ohigh = owner(y, x, core)
    mine = (oy == y) & (ocore == core)
    low = low_block(y, core)
    sib = low + 1 - 2 * (low % 2)
    far = low + 2 - 4 * (low // 2)
    farsib = sib + 2 - 4 * (sib // 2)
    partner = seq + 32 - 64 * (y % 2)
    before = (seq + 127) % 128
    after = (seq + 1) % 128
    head = x * 8 + z

    load_bytes = pltpu.make_async_copy(states, bytes_in, s_load.at[0])
    load_cot = pltpu.make_async_copy(cot_rows, cot, s_load.at[1])
    load_bytes.start()
    load_cot.start()

    barrier = pltpu.get_barrier_semaphore()

    def greet(i, _):
        s, d, _row = source(y, core, (i + head) % 32)

        @pl.when((s != seq) | (d != core))
        def _():
            signal(barrier, s, d)

        return 0

    lax.fori_loop(0, 32, greet, 0)

    def greet_column(i, _):
        c = (y * 2 + core + i) % 8
        signal(barrier, (c // 2) * 32 + head, c % 2)
        return 0

    lax.fori_loop(1, 8, greet_column, 0)
    signal(barrier, after, core)

    base = seq * 128
    start = column(starts[...], PIECE) - base
    length = column(lengths[...], PIECE)
    at_byte = lax.broadcasted_iota(jnp.int32, (PIECE, 128), 1)
    member = ((at_byte >= start) & (at_byte < start + length)).astype(f32).astype(bf16)
    first = starts[:, 0:1] - base
    lead = (lax.broadcasted_iota(jnp.int32, (16, 128), 1) < first).astype(f32).astype(bf16)
    inverse = 1.0 / length.astype(f32)
    load_bytes.wait()
    spill[...] = jnp.dot(lead, bytes_in[...], preferred_element_type=f32)[0:1, :]
    sums[...] = jnp.dot(member, bytes_in[...], preferred_element_type=f32) * inverse

    @pl.when(mine)
    def _():
        pl.semaphore_wait(barrier, 31 + 7 + 1)

    @pl.when(jnp.logical_not(mine))
    def _():
        pl.semaphore_wait(barrier, 32 + 7 + 1)

    spilling = remote(spill, spill_in, s_spill, r_spill, before, core)
    spilling.start()

    def scatter_rows(src, dst, row, first_row, count, send, recv):
        def step(i, _):
            h = head_at(x, z, i)
            part = src.at[pl.ds(first_row, count), pl.ds(pl.multiple_of(h * HEAD_DIM, HEAD_DIM), HEAD_DIM)]
            there = dst.at[pl.ds(pl.multiple_of(row + first_row, 16), count), :]
            target = oy * 32 + h
            local = (target == seq) & (ocore == core)

            @pl.when(local)
            def _():
                pltpu.make_async_copy(part, there, recv).start()

            @pl.when(jnp.logical_not(local))
            def _():
                remote(part, there, send, recv, target, ocore).start()

            return 0

        lax.fori_loop(0, 32, step, 0)

    pooled[0:16, :] = sums[0:16, :].astype(bf16)
    scatter_rows(pooled, kfull, seq * PIECE, 0, 16, s_pool, r_pool)
    spilling.wait_recv()
    last = (lax.broadcasted_iota(jnp.int32, (16, 1), 0) == 15) & (seq < 127)
    pooled[16:32, :] = (sums[16:32, :] + jnp.where(last, spill_in[...] * inverse[16:32, :], 0.0)).astype(bf16)
    scatter_rows(pooled, kfull, seq * PIECE, 16, 16, s_pool, r_pool)
    load_cot.wait()
    scatter_rows(cot, cot_h, ohigh * BLOCK + (seq % 16) * PIECE, 0, PIECE, s_cot, r_cot)

    qgain = qgain_all[pl.ds(head, 1), :]
    kgain = kgain_all[pl.ds(head, 1), :]

    def clear(j, _):
        dk[chunk(j), :] = jnp.zeros((BLOCK, HEAD_DIM), f32)
        dv[chunk(j), :] = jnp.zeros((BLOCK, HEAD_DIM), f32)
        return 0

    lax.fori_loop(0, 8, clear, 0)

    pltpu.make_async_copy(kfull.at[pl.ds(0, 1024), :], kfull.at[pl.ds(0, 1024), :], r_pool).wait()
    across, beside = [], []
    for i, block in enumerate((low, 7 - low)):
        there = kfull.at[chunk(block), :]
        across.append(remote(there, there, s_key.at[i], r_key.at[i], partner, core))
        beside.append(remote(there, there, s_key.at[2 + i], r_key.at[2 + i], seq, 1 - core))
        across[i].start()
        beside[i].start()

    def prepare(block):
        keyed[chunk(block), :] = (kfull[chunk(block), :].astype(f32) * kgain).astype(bf16)

    for i, block in enumerate((low, 7 - low)):
        query[chunk(i), :] = (kfull[chunk(block), :].astype(f32) * qgain).astype(bf16)
        prepare(block)

    relays = []

    def other_keys():
        for i, block in enumerate((sib, 7 - sib)):
            beside[i].wait_recv()
            prepare(block)
        for i, block in enumerate((far, 7 - far)):
            across[i].wait_recv()
            there = kfull.at[chunk(block), :]
            relays.append(remote(there, there, s_key.at[4 + i], r_key.at[4 + i], seq, 1 - core))
            relays[i].start()
            prepare(block)
        for i, block in enumerate((farsib, 7 - farsib)):
            relays[i].wait_recv()
            prepare(block)

    forward(low, kfull, keyed, query, s_ref, w_ref, stat, mixed, other_keys)
    rs = normed(mixed, out_h)

    head_columns = pl.ds(pl.multiple_of(head * HEAD_DIM, HEAD_DIM), HEAD_DIM)

    def scatter_back(src, dst, send, recv):
        def step(i, _):
            s, d, row = source(y, core, (i + head) % 32)
            part = src.at[pl.ds(pl.multiple_of(row, PIECE), PIECE), :]
            there = dst.at[:, head_columns]
            local = (s == seq) & (d == core)

            @pl.when(local)
            def _():
                pltpu.make_async_copy(part, there, recv).start()

            @pl.when(jnp.logical_not(local))
            def _():
                remote(part, there, send, recv, s, d).start()

            return 0

        lax.fori_loop(0, 32, step, 0)

    scatter_back(out_h, patch_out, s_out, r_out)
    pltpu.make_async_copy(cot_h, cot_h, r_cot).wait()
    g = cot_h[...].astype(f32)
    m = mixed[...]
    dmb[...] = (g * rs - m * (jnp.sum(g * m, -1, keepdims=True) * (rs * rs * rs) * (1.0 / HEAD_DIM))).astype(bf16)
    backward(low, kfull, keyed, query, dmb, s_ref, w_ref, d_ref, stat, delta, dk, dv, dq)

    gk = jnp.zeros((1, HEAD_DIM), f32)
    to_sib = []
    for i, block in enumerate((farsib, 7 - farsib, sib, 7 - sib, far, 7 - far, low, 7 - low)):
        d = dk[chunk(block), :]
        dv[chunk(block), :] += d * kgain
        gk = gk + jnp.sum(d * kfull[chunk(block), :].astype(f32), 0, keepdims=True)
        if i < 4:
            to_sib.append(remote(dv.at[chunk(block), :], from_sib.at[i], s_sib.at[i], r_sib.at[i], seq, 1 - core))
            to_sib[i].start()
    gq = jnp.zeros((1, HEAD_DIM), f32)
    for i, block in enumerate((low, 7 - low)):
        gq = gq + jnp.sum(dq[chunk(i), :] * kfull[chunk(block), :].astype(f32), 0, keepdims=True)
    place_in_column = pl.ds(y * 2 + core, 1)
    column_in[place_in_column] = jnp.concatenate([gq, gk], 0)[None]

    def send_column(i, _):
        c = (y * 2 + core + i) % 8
        slot = column_in.at[place_in_column]
        remote(slot, slot, s_col, r_col, (c // 2) * 32 + head, c % 2).start()
        return 0

    lax.fori_loop(1, 8, send_column, 0)

    to_partner = []
    for i, block in enumerate((far, 7 - far)):
        to_sib[i].wait_recv()
        to_far[i] = (dv[chunk(block), :] + from_sib[i]).astype(bf16)
        to_partner.append(remote(to_far.at[i], from_far.at[i], s_far.at[i], r_far.at[i], partner, core))
        to_partner[i].start()
    for i, block in enumerate((low, 7 - low)):
        to_sib[2 + i].wait_recv()
        mixed[chunk(i), :] = dv[chunk(block), :] + from_sib[2 + i] + dq[chunk(i), :] * qgain

    pltpu.make_async_copy(column_in.at[0:7], column_in.at[0:7], r_col).wait()
    total = column_in[0]
    for i in range(1, 8):
        total = total + column_in[i]
    pltpu.make_async_copy(column_in.at[0:7], column_in.at[0:7], s_col).wait()
    column_in[place_in_column] = total[None]

    def send_plane(i, _):
        s, d, _row = source(y, core, (i + head) % 32)
        part = column_in.at[place_in_column]
        there = plane.at[pl.ds(head, 1)]
        local = (s == seq) & (d == core)

        @pl.when(local)
        def _():
            pltpu.make_async_copy(part, there, r_pla).start()

        @pl.when(jnp.logical_not(local))
        def _():
            remote(part, there, s_pla, r_pla, s, d).start()

        return 0

    lax.fori_loop(0, 32, send_plane, 0)

    for i in range(2):
        to_partner[i].wait_recv()
        mine_b[chunk(i), :] = (mixed[chunk(i), :] + from_far[i].astype(f32)).astype(bf16)
    scatter_back(mine_b, dpool, s_dp, r_dp)

    pltpu.make_async_copy(dpool, dpool, r_dp).wait()
    back[...] = dpool[16:32, :].astype(f32)[15:16, :] * inverse[PIECE - 1:PIECE, :]
    returning = remote(back, spill_back, s_back, r_back, after, core)
    returning.start()
    returning.wait_recv()

    pltpu.make_async_copy(patch_out, patch_out, r_out).wait()
    pltpu.make_async_copy(plane, plane, r_pla).wait()
    returning.wait_send()
    spilling.wait_send()
    for copy in across + beside + relays + to_sib + to_partner:
        copy.wait_send()

    @pl.when(mine)
    def _():
        for src, sem in ((pooled, s_pool), (cot, s_cot)):
            part = src.at[:, pl.ds(0, 31 * HEAD_DIM)]
            pltpu.make_async_copy(part, part, sem).wait()
        for src, sem in ((out_h, s_out), (mine_b, s_dp)):
            part = src.at[0:31 * PIECE]
            pltpu.make_async_copy(part, part, sem).wait()
        pltpu.make_async_copy(plane.at[0:31], plane.at[0:31], s_pla).wait()

    @pl.when(jnp.logical_not(mine))
    def _():
        for src, sem in ((pooled, s_pool), (cot, s_cot), (out_h, s_out), (mine_b, s_dp), (plane, s_pla)):
            pltpu.make_async_copy(src, src, sem).wait()


def finish(starts, lengths, dpool, spill_back, out_in, plane, grad, patch_out, gq, gk):
    base = lax.axis_index("seq") * 128
    start = starts[...] - base
    length = lengths[...]
    at_byte = lax.broadcasted_iota(jnp.int32, (128, PIECE), 0)
    inside = (at_byte >= start) & (at_byte < start + length)
    member = inside.astype(f32).astype(bf16)
    by_byte = jnp.sum(jnp.where(inside, 1.0 / length.astype(f32), 0.0), 1, keepdims=True)
    lead = lax.broadcasted_iota(jnp.int32, (8, 1), 0) < start[:, 0:1]
    grad[...] = jnp.dot(member, dpool[...], preferred_element_type=f32) * by_byte
    grad[0:8, :] = jnp.where(lead, spill_back[...], grad[0:8, :])
    patch_out[...] = out_in[...]

    @pl.when(pl.program_id(0) == 0)
    def _():
        for i in range(HEADS):
            gq[i:i + 1, :] = plane[i, 0:1, :]
            gk[i:i + 1, :] = plane[i, 1:2, :]


VMEM = pl.BlockSpec(memory_space=pltpu.VMEM)
ANY = pl.BlockSpec(memory_space=pl.ANY)
DMA = pltpu.SemaphoreType.DMA
PARTS = 4


def shape(dims, dtype):
    return jax.ShapeDtypeStruct(dims, dtype)


def on_device(byte_states, patch_starts, patch_lengths, query_gain, key_gain, out_cotangent):
    states = byte_states[0]
    cot = out_cotangent[0]
    width = states.shape[1]
    own = 2 * BLOCK
    keys = 8 * BLOCK
    V = pltpu.VMEM
    out_rows, dpool, spill_back, plane = pl.pallas_call(
        whole,
        out_shape=(shape((PIECE, width), bf16), shape((PIECE, width), bf16), shape((1, width), f32),
                   shape((HEADS, 2, HEAD_DIM), f32)),
        in_specs=[ANY, VMEM, VMEM, VMEM, VMEM, ANY],
        out_specs=(VMEM,) * 4,
        scratch_shapes=[
            V((128, width), bf16), V((PIECE, width), bf16), V((PIECE, width), bf16), V((PIECE, width), f32),
            V((1, width), f32), V((1, width), f32), V((1, width), f32),
            V((keys, HEAD_DIM), bf16), V((own, HEAD_DIM), bf16), V((own, HEAD_DIM), bf16),
            V((keys, HEAD_DIM), bf16), V((own, HEAD_DIM), bf16),
            V((BLOCK, STEPS * BLOCK), f32), V((BLOCK, STEPS * BLOCK), bf16), V((BLOCK, STEPS * BLOCK), f32),
            V((keys, HEAD_DIM), f32), V((keys, HEAD_DIM), f32),
            V((own, HEAD_DIM), f32), V((own, HEAD_DIM), f32), V((own, HEAD_DIM), f32), V((own, HEAD_DIM), f32),
            V((own, HEAD_DIM), bf16),
            V((4, BLOCK, HEAD_DIM), f32), V((2, BLOCK, HEAD_DIM), bf16), V((2, BLOCK, HEAD_DIM), bf16),
            V((own, HEAD_DIM), bf16), V((8, 2, HEAD_DIM), f32),
            DMA((2,)), DMA, DMA, DMA, DMA, DMA, DMA, DMA((6,)), DMA((6,)),
            DMA, DMA, DMA((4,)), DMA((4,)), DMA((2,)), DMA((2,)), DMA, DMA, DMA, DMA, DMA, DMA,
            DMA, DMA,
        ],
        compiler_params=pltpu.CompilerParams(
            collective_id=0, has_side_effects=True, vmem_limit_bytes=56 << 20
        ),
    )(states, patch_starts, patch_lengths, query_gain.reshape(HEADS, HEAD_DIM), key_gain.reshape(HEADS, HEAD_DIM), cot)
    part = width // PARTS

    def columns(rows):
        return pl.BlockSpec((rows, part), lambda i: (0, i))

    grad, patch_out, gq, gk = pl.pallas_call(
        finish,
        grid=(PARTS,),
        out_shape=(shape((128, width), f32), shape((PIECE, width), bf16),
                   shape((HEADS, HEAD_DIM), f32), shape((HEADS, HEAD_DIM), f32)),
        in_specs=[VMEM, VMEM, columns(PIECE), columns(1), columns(PIECE), VMEM],
        out_specs=(columns(128), columns(PIECE), VMEM, VMEM),
        compiler_params=pltpu.CompilerParams(vmem_limit_bytes=16 << 20),
    )(patch_starts, patch_lengths, dpool, spill_back, out_rows, plane)
    return patch_out[None], grad[None], gq.reshape(width), gk.reshape(width)


def solution(mesh):
    rows = P("dp", "seq", None)
    flat = P("dp", "seq")
    return jax.shard_map(
        on_device,
        mesh=mesh,
        in_specs=(rows, flat, flat, P(), P(), rows),
        out_specs=(rows, rows, P(), P()),
        check_vma=False,
    )
```

```python
import functools
import math

import jax
import jax.numpy as jnp
from jax import lax
from jax.experimental import pallas as pl
from jax.experimental.pallas import tpu as pltpu
from jax.sharding import PartitionSpec as P

f32 = jnp.float32
bf16 = jnp.bfloat16
HEAD_DIM = 128
HEADS = 32
PIECE = 32
BLOCK = 512
EPS = 1e-6
NT = (((1,), (1,)), ((), ()))
TN = (((0,), (0,)), ((), ()))


def place():
    seq = lax.axis_index("seq")
    core = lax.axis_index("dp")
    y = seq // 32
    return seq, core, y, (seq // 8) % 4, seq % 8


def at(seq, core):
    return {"seq": seq, "dp": core}


def low_block(y, core):
    return core + 2 * (((y + 1) // 2) % 2)


def owner(y, x, doc):
    block = 2 * y + x // 2
    high = block // 4
    low = block + high * (7 - 2 * block)
    half = low // 2
    return (doc * (3 - half) + (1 - doc) * half), low % 2, high


def source(y, core, i):
    low = low_block(y, core)
    high = i // 16
    block = low + high * (7 - 2 * low)
    return block * 16 + i % 16, y // 2, i * PIECE


def head_at(x, z, i):
    return ((x + i // 8) % 4) * 8 + (z + i % 8) % 8


MESH = pl.DeviceIdType.MESH


def signal(sem, seq, core):
    pl.semaphore_signal(sem, inc=1, device_id=at(seq, core), device_id_type=MESH)


def remote(src, dst, send, recv, seq, core):
    return pltpu.make_async_remote_copy(
        src_ref=src, dst_ref=dst, send_sem=send, recv_sem=recv,
        device_id=at(seq, core), device_id_type=MESH,
    )


def column(row, count):
    r = lax.broadcasted_iota(jnp.int32, (count, count), 0)
    c = lax.broadcasted_iota(jnp.int32, (count, count), 1)
    return jnp.sum(jnp.where(r == c, jnp.broadcast_to(row, (count, count)), 0), 1, keepdims=True)


SCALE = HEAD_DIM ** -0.5
C2 = SCALE * math.log2(math.e)
STEPS = 9
GROUP = BLOCK // HEAD_DIM


def chunk(j):
    return pl.ds(pl.multiple_of(j * BLOCK, BLOCK), BLOCK)


def lanes(x, op):
    parts = [x[:, g * HEAD_DIM:(g + 1) * HEAD_DIM] for g in range(x.shape[1] // HEAD_DIM)]
    return functools.reduce(op, parts)


def step_at(low, t):
    if isinstance(t, int) and t in (0, 7, 8):
        return {0: (0, low), 7: (1, low), 8: (1, 7 - low)}[t]
    mask = 3 - (t - 1) // 2
    second = (t - 1) % 2
    odd, far = mask % 2, mask // 2
    chunk_low = (low + odd) % 2 + 2 * ((low // 2 + far) % 2)
    mirrored = second * (far * (1 - low // 2) + (1 - far) * (1 - low % 2))
    return 1 - second + mirrored, chunk_low + mirrored * (7 - 2 * chunk_low)


def over_steps(body, between=None):
    body((0, 8, 7))
    if between is not None:
        between()

    def three(i, _):
        body(tuple(1 + 3 * i + u for u in range(3)))
        return 0

    lax.fori_loop(0, 2, three, 0)


def tiled(x):
    return jnp.concatenate([x] * GROUP, 1)


def forward(low, values, keyed, query, s_ref, w_ref, stat, mixed, between):
    stat[...] = jnp.full(stat.shape, -1e30, f32)

    def cols(t):
        return pl.ds(pl.multiple_of(t * BLOCK, BLOCK), BLOCK)

    def scores(steps):
        for t in steps:
            high, j = step_at(low, t)
            s = lax.dot_general(query[chunk(high), :], keyed[chunk(j), :], NT, preferred_element_type=f32)
            if isinstance(t, int) and t != 7:
                r = lax.broadcasted_iota(jnp.int32, s.shape, 0)
                c = lax.broadcasted_iota(jnp.int32, s.shape, 1)
                s = jnp.where(c <= r, s, -1e30)
            s_ref[:, cols(t)] = s
            stat[chunk(high), :] = jnp.maximum(stat[chunk(high), :], lanes(s, jnp.maximum))

    over_steps(scores, between)
    stat[...] = jnp.broadcast_to(jnp.max(stat[...], -1, keepdims=True), stat.shape)
    mixed[...] = jnp.zeros(mixed.shape, f32)

    def expo(steps):
        for t in steps:
            high, j = step_at(low, t)
            e = jnp.exp2((s_ref[:, cols(t)] - tiled(stat[chunk(high), :])) * C2)
            s_ref[:, cols(t)] = e
            mixed[chunk(high), :] += lanes(e, jnp.add)

    over_steps(expo)
    stat[...] = jnp.broadcast_to(1.0 / jnp.sum(mixed[...], -1, keepdims=True), stat.shape)
    mixed[...] = jnp.zeros(mixed.shape, f32)

    def mix(steps):
        for t in steps:
            high, j = step_at(low, t)
            w = (s_ref[:, cols(t)] * tiled(stat[chunk(high), :])).astype(bf16)
            w_ref[:, cols(t)] = w
            mixed[chunk(high), :] += jnp.dot(w, values(j), preferred_element_type=f32)

    over_steps(mix)


def normed(mixed, out):
    m = mixed[...]
    rs = 1.0 / jnp.sqrt(jnp.mean(m * m, -1, keepdims=True) + EPS)
    out[...] = (m * rs).astype(bf16)
    return rs


def backward(low, values, keyed, query, dmb, s_ref, w_ref, d_ref, stat, delta, dk, dv, dq, after):
    def cols(t):
        return pl.ds(pl.multiple_of(t * BLOCK, BLOCK), BLOCK)

    delta[...] = jnp.zeros(delta.shape, f32)

    def dprobs(steps):
        for t in steps:
            high, j = step_at(low, t)
            dp = lax.dot_general(dmb[chunk(high), :], values(j), NT, preferred_element_type=f32)
            d_ref[:, cols(t)] = dp
            dv[chunk(j), :] += lax.dot_general(w_ref[:, cols(t)], dmb[chunk(high), :], TN, preferred_element_type=f32)
            delta[chunk(high), :] += lanes(dp * s_ref[:, cols(t)], jnp.add)

    over_steps(dprobs)
    delta[...] = jnp.broadcast_to(jnp.sum(delta[...], -1, keepdims=True), delta.shape) * stat[...]
    stat[...] = stat[...] * SCALE
    dq[...] = jnp.zeros(dq.shape, f32)

    def back(steps):
        for t in steps:
            high, j = step_at(low, t)
            ds = ((s_ref[:, cols(t)] * tiled(stat[chunk(high), :]))
                  * (d_ref[:, cols(t)] - tiled(delta[chunk(high), :]))).astype(bf16)
            dk[chunk(j), :] += lax.dot_general(ds, query[chunk(high), :], TN, preferred_element_type=f32)
            dq[chunk(high), :] += jnp.dot(ds, keyed[chunk(j), :], preferred_element_type=f32)

    for n, steps in enumerate(((1, 2), (3, 4), (5, 6), (0, 8, 7))):
        back(steps)
        after(n)


def whole(states, starts, lengths, qgain_all, kgain_all, cot_rows,
          patch_out, dpool, spill_back, plane, inverse_before,
          bytes_in, cot, pooled, sums, spill, spill_in, inverse_out, kfull, cot_h, out_h,
          keyed, query, s_ref, w_ref, d_ref, dk, dv, dq, stat, delta, mixed, dmb,
          from_sib, to_far, from_far, mine_b, last_rows, column_in,
          s_load, s_spill, r_spill, s_pool, r_pool, s_cot, r_cot, s_key, r_key,
          s_out, r_out, s_sib, r_sib, s_far, r_far, s_dp, r_dp, s_col, r_col, s_pla, r_pla,
          s_last, r_last, s_inv, r_inv):
    seq, core, y, x, z = place()
    oy, ocore, ohigh = owner(y, x, core)
    mine = (oy == y) & (ocore == core)
    low = low_block(y, core)
    sib = low + 1 - 2 * (low % 2)
    far = low + 2 - 4 * (low // 2)
    farsib = sib + 2 - 4 * (sib // 2)
    partner = seq + 32 - 64 * (y % 2)
    before = (seq + 127) % 128
    after = (seq + 1) % 128
    head = x * 8 + z
    by, bcore, _high = owner(before // 32, (before // 8) % 4, core)
    mine_before = (by == y) & (bcore == core)
    pending = []

    def wait_all(ref, sem):
        pltpu.make_async_copy(ref, ref, sem).wait()

    def sent(ref, part, sem, own=mine):
        @pl.when(own)
        def _():
            wait_all(part, sem)

        @pl.when(jnp.logical_not(own))
        def _():
            wait_all(ref, sem)

    load_bytes = pltpu.make_async_copy(states, bytes_in, s_load.at[0])
    load_cot = pltpu.make_async_copy(cot_rows, cot, s_load.at[1])
    load_bytes.start()
    load_cot.start()

    barrier = pltpu.get_barrier_semaphore()

    def greet(i, _):
        s, d, _row = source(y, core, (i + head) % 32)

        @pl.when((s != seq) | (d != core))
        def _():
            signal(barrier, s, d)

        return 0

    lax.fori_loop(0, 32, greet, 0)

    def greet_column(i, _):
        c = (y * 2 + core + i) % 8
        signal(barrier, (c // 2) * 32 + head, c % 2)
        return 0

    lax.fori_loop(1, 8, greet_column, 0)
    signal(barrier, after, core)
    signal(barrier, before, core)

    base = seq * 128
    start = column(starts[...], PIECE) - base
    length = column(lengths[...], PIECE)
    at_byte = lax.broadcasted_iota(jnp.int32, (PIECE, 128), 1)
    member = ((at_byte >= start) & (at_byte < start + length)).astype(f32).astype(bf16)
    first = starts[:, 0:1] - base
    lead = (lax.broadcasted_iota(jnp.int32, (16, 128), 1) < first).astype(f32).astype(bf16)
    inverse = 1.0 / length.astype(f32)
    inverse_out[...] = jnp.broadcast_to(inverse[PIECE - 1:PIECE, :], (1, HEAD_DIM))
    load_bytes.wait()
    spill[...] = jnp.dot(lead, bytes_in[...], preferred_element_type=f32)[0:1, :]
    sums[...] = jnp.dot(member, bytes_in[...], preferred_element_type=f32) * inverse

    @pl.when(mine)
    def _():
        pl.semaphore_wait(barrier, 31 + 7 + 2)

    @pl.when(jnp.logical_not(mine))
    def _():
        pl.semaphore_wait(barrier, 32 + 7 + 2)

    spilling = remote(spill, spill_in, s_spill, r_spill, before, core)
    spilling.start()
    telling = remote(inverse_out, inverse_before, s_inv, r_inv, after, core)
    telling.start()
    pending.extend([spilling.wait_send, telling.wait])

    def scatter_rows(src, dst, first_row, count, send, recv):
        def step(i, _):
            h = head_at(x, z, i)
            part = src.at[pl.ds(first_row, count), pl.ds(pl.multiple_of(h * HEAD_DIM, HEAD_DIM), HEAD_DIM)]
            target = oy * 32 + h
            local = (target == seq) & (ocore == core)

            @pl.when(local)
            def _():
                pltpu.make_async_copy(part, dst, recv).start()

            @pl.when(jnp.logical_not(local))
            def _():
                remote(part, dst, send, recv, target, ocore).start()

            return 0

        lax.fori_loop(0, 32, step, 0)

    columns = pl.ds(0, 31 * HEAD_DIM)
    pooled[0:16, :] = sums[0:16, :].astype(bf16)
    scatter_rows(pooled, kfull.at[seq, pl.ds(0, 16), :], 0, 16, s_pool.at[0], r_pool.at[0])
    spilling.wait_recv()
    last = (lax.broadcasted_iota(jnp.int32, (16, 1), 0) == 15) & (seq < 127)
    pooled[16:32, :] = (sums[16:32, :] + jnp.where(last, spill_in[...] * inverse[16:32, :], 0.0)).astype(bf16)
    scatter_rows(pooled, kfull.at[seq, pl.ds(16, 16), :], 16, 16, s_pool.at[1], r_pool.at[1])
    load_cot.wait()
    crow = pl.multiple_of(ohigh * BLOCK + (seq % 16) * PIECE, PIECE)
    scatter_rows(cot, cot_h.at[pl.ds(crow, PIECE), :], 0, PIECE, s_cot, r_cot)
    for i in range(2):
        half = pooled.at[pl.ds(16 * i, 16), :]
        pending.append(functools.partial(sent, half, half.at[:, columns], s_pool.at[i]))
    pending.append(functools.partial(sent, cot, cot.at[:, columns], s_cot))

    qgain = qgain_all[pl.ds(head, 1), :]
    kgain = kgain_all[pl.ds(head, 1), :]

    def clear(j, _):
        dk[chunk(j), :] = jnp.zeros((BLOCK, HEAD_DIM), f32)
        dv[chunk(j), :] = jnp.zeros((BLOCK, HEAD_DIM), f32)
        return 0

    lax.fori_loop(0, 8, clear, 0)

    def pieces(block):
        return pl.ds(block * 16, 16)

    def values(block):
        return kfull[pieces(block)].reshape(BLOCK, HEAD_DIM)

    def prepare(block):
        keyed[chunk(block), :] = (values(block).astype(f32) * kgain).astype(bf16)

    across, beside, relays = {}, {}, {}
    for half in range(2):
        rows = pl.ds(16 * half, 16)
        wait_all(kfull.at[pl.ds(0, 32), rows, :], r_pool.at[half])
        for i, block in enumerate((low, 7 - low)):
            n = 2 * half + i
            there = kfull.at[pieces(block), rows, :]
            across[n] = remote(there, there, s_key.at[n], r_key.at[n], partner, core)
            across[n].start()
            beside[n] = remote(there, there, s_key.at[4 + n], r_key.at[4 + n], seq, 1 - core)
            beside[n].start()
            pending.extend([across[n].wait_send, beside[n].wait_send])
    for i, block in enumerate((low, 7 - low)):
        query[chunk(i), :] = (values(block).astype(f32) * qgain).astype(bf16)
        prepare(block)

    def other_keys():
        for n in range(4):
            block = (far, 7 - far)[n % 2]
            across[n].wait_recv()
            there = kfull.at[pieces(block), pl.ds(16 * (n // 2), 16), :]
            relays[n] = remote(there, there, s_key.at[8 + n], r_key.at[8 + n], seq, 1 - core)
            relays[n].start()
            pending.append(relays[n].wait_send)
            beside[n].wait_recv()
        for block in (sib, 7 - sib, far, 7 - far):
            prepare(block)
        for n in range(4):
            relays[n].wait_recv()
        for block in (farsib, 7 - farsib):
            prepare(block)

    forward(low, values, keyed, query, s_ref, w_ref, stat, mixed, other_keys)
    rs = normed(mixed, out_h)

    head_columns = pl.ds(pl.multiple_of(head * HEAD_DIM, HEAD_DIM), HEAD_DIM)

    def scatter_back(first, count, part_of, there, send, recv, shift=0):
        def step(i, _):
            n = first + (i + head) % count
            s, d, row = source(y, core, n)
            s = (s + shift) % 128
            part = part_of(n)
            local = (s == seq) & (d == core)

            @pl.when(local)
            def _():
                pltpu.make_async_copy(part, there, recv).start()

            @pl.when(jnp.logical_not(local))
            def _():
                remote(part, there, send, recv, s, d).start()

            return 0

        lax.fori_loop(0, count, step, 0)

    def rows_of(ref):
        return lambda n: ref.at[pl.ds(pl.multiple_of(n * PIECE, PIECE), PIECE), :]

    scatter_back(0, 32, rows_of(out_h), patch_out.at[:, head_columns], s_out, r_out)
    pending.append(functools.partial(sent, out_h, out_h.at[0:31 * PIECE], s_out))
    pending.append(functools.partial(wait_all, patch_out, r_out))
    wait_all(cot_h, r_cot)
    g = cot_h[...].astype(f32)
    m = mixed[...]
    dmb[...] = (g * rs - m * (jnp.sum(g * m, -1, keepdims=True) * (rs * rs * rs) * (1.0 / HEAD_DIM))).astype(bf16)

    gk = [jnp.zeros((1, HEAD_DIM), f32)]
    to_sib, to_partner = [], []

    def complete(block):
        d = dk[chunk(block), :]
        dv[chunk(block), :] += d * kgain
        gk[0] = gk[0] + jnp.sum(d * values(block).astype(f32), 0, keepdims=True)

    def give_sib(block):
        i = len(to_sib)
        to_sib.append(remote(dv.at[chunk(block), :], from_sib.at[i], s_sib.at[i], r_sib.at[i], seq, 1 - core))
        to_sib[i].start()
        pending.append(to_sib[i].wait_send)

    def after_steps(n):
        blocks = ((farsib, 7 - farsib), (far, 7 - far), (sib, 7 - sib), (low, 7 - low))[n]
        for i, block in enumerate(blocks):
            complete(block)
            if n in (0, 2):
                give_sib(block)
            if n == 1:
                to_sib[i].wait_recv()
                to_far[i] = (dv[chunk(block), :] + from_sib[i]).astype(bf16)
                to_partner.append(remote(to_far.at[i], from_far.at[i], s_far.at[i], r_far.at[i], partner, core))
                to_partner[i].start()
                pending.append(to_partner[i].wait_send)

    backward(low, values, keyed, query, dmb, s_ref, w_ref, d_ref, stat, delta, dk, dv, dq, after_steps)
    for i, block in enumerate((low, 7 - low)):
        to_sib[2 + i].wait_recv()
        to_partner[i].wait_recv()
        mixed[chunk(i), :] = (dv[chunk(block), :] + from_sib[2 + i] + dq[chunk(i), :] * qgain
                              + from_far[i].astype(f32))
        mine_b[chunk(i), :] = mixed[chunk(i), :].astype(bf16)
        scatter_back(16 * i, 16, rows_of(mine_b), dpool.at[:, head_columns], s_dp, r_dp)
    pending.append(functools.partial(sent, mine_b, mine_b.at[0:31 * PIECE], s_dp))

    for i in range(32):
        last_rows[i] = mixed[i * PIECE + PIECE - 1:(i + 1) * PIECE, :]
    scatter_back(0, 32, lambda n: last_rows.at[n], spill_back.at[:, head_columns], s_last, r_last, 1)
    pending.append(functools.partial(sent, last_rows, last_rows.at[0:31], s_last, mine_before))

    gq = jnp.zeros((1, HEAD_DIM), f32)
    for i, block in enumerate((low, 7 - low)):
        gq = gq + jnp.sum(dq[chunk(i), :] * values(block).astype(f32), 0, keepdims=True)
    place_in_column = pl.ds(y * 2 + core, 1)
    column_in[place_in_column] = jnp.concatenate([gq, gk[0]], 0)[None]

    def send_column(i, _):
        c = (y * 2 + core + i) % 8
        slot = column_in.at[place_in_column]
        remote(slot, slot, s_col, r_col, (c // 2) * 32 + head, c % 2).start()
        return 0

    lax.fori_loop(1, 8, send_column, 0)
    wait_all(column_in.at[0:7], r_col)
    total = column_in[0]
    for i in range(1, 8):
        total = total + column_in[i]
    wait_all(column_in.at[0:7], s_col)
    column_in[place_in_column] = total[None]
    scatter_back(0, 32, lambda n: column_in.at[y * 2 + core], plane.at[head], s_pla, r_pla)
    pending.append(functools.partial(sent, plane, plane.at[0:31], s_pla))
    wait_all(dpool, r_dp)
    wait_all(spill_back, r_last)
    wait_all(plane, r_pla)
    for wait in pending:
        wait()


def finish(starts, lengths, dpool, spill_back, inverse_before, out_in, plane, grad, patch_out, gq, gk):
    base = lax.axis_index("seq") * 128
    start = starts[...] - base
    length = lengths[...]
    at_byte = lax.broadcasted_iota(jnp.int32, (128, PIECE), 0)
    inside = (at_byte >= start) & (at_byte < start + length)
    member = inside.astype(f32).astype(bf16)
    by_byte = jnp.sum(jnp.where(inside, 1.0 / length.astype(f32), 0.0), 1, keepdims=True)
    lead = lax.broadcasted_iota(jnp.int32, (8, 1), 0) < start[:, 0:1]
    grad[...] = jnp.dot(member, dpool[...], preferred_element_type=f32) * by_byte
    grad[0:8, :] = jnp.where(lead, spill_back[...] * inverse_before[:, 0:1], grad[0:8, :])
    patch_out[...] = out_in[...]

    @pl.when(pl.program_id(0) == 0)
    def _():
        for i in range(HEADS):
            gq[i:i + 1, :] = plane[i, 0:1, :]
            gk[i:i + 1, :] = plane[i, 1:2, :]


VMEM = pl.BlockSpec(memory_space=pltpu.VMEM)
ANY = pl.BlockSpec(memory_space=pl.ANY)
DMA = pltpu.SemaphoreType.DMA
PARTS = 4


def shape(dims, dtype):
    return jax.ShapeDtypeStruct(dims, dtype)


def on_device(byte_states, patch_starts, patch_lengths, query_gain, key_gain, out_cotangent):
    states = byte_states[0]
    cot = out_cotangent[0]
    width = states.shape[1]
    own = 2 * BLOCK
    keys = 8 * BLOCK
    V = pltpu.VMEM
    out_rows, dpool, spill_back, plane, inverse_before = pl.pallas_call(
        whole,
        out_shape=(shape((PIECE, width), bf16), shape((PIECE, width), bf16), shape((1, width), f32),
                   shape((HEADS, 2, HEAD_DIM), f32), shape((1, HEAD_DIM), f32)),
        in_specs=[ANY, VMEM, VMEM, VMEM, VMEM, ANY],
        out_specs=(VMEM,) * 5,
        scratch_shapes=[
            V((128, width), bf16), V((PIECE, width), bf16), V((PIECE, width), bf16), V((PIECE, width), f32),
            V((1, width), f32), V((1, width), f32), V((1, HEAD_DIM), f32),
            V((128, PIECE, HEAD_DIM), bf16), V((own, HEAD_DIM), bf16), V((own, HEAD_DIM), bf16),
            V((keys, HEAD_DIM), bf16), V((own, HEAD_DIM), bf16),
            V((BLOCK, STEPS * BLOCK), f32), V((BLOCK, STEPS * BLOCK), bf16), V((BLOCK, STEPS * BLOCK), f32),
            V((keys, HEAD_DIM), f32), V((keys, HEAD_DIM), f32),
            V((own, HEAD_DIM), f32), V((own, HEAD_DIM), f32), V((own, HEAD_DIM), f32), V((own, HEAD_DIM), f32),
            V((own, HEAD_DIM), bf16),
            V((4, BLOCK, HEAD_DIM), f32), V((2, BLOCK, HEAD_DIM), bf16), V((2, BLOCK, HEAD_DIM), bf16),
            V((own, HEAD_DIM), bf16), V((HEADS, 1, HEAD_DIM), f32), V((8, 2, HEAD_DIM), f32),
            DMA((2,)), DMA, DMA, DMA((2,)), DMA((2,)), DMA, DMA, DMA((12,)), DMA((12,)),
            DMA, DMA, DMA((4,)), DMA((4,)), DMA((2,)), DMA((2,)), DMA, DMA, DMA, DMA, DMA, DMA,
            DMA, DMA, DMA, DMA,
        ],
        compiler_params=pltpu.CompilerParams(
            collective_id=0, has_side_effects=True, vmem_limit_bytes=56 << 20
        ),
    )(states, patch_starts, patch_lengths, query_gain.reshape(HEADS, HEAD_DIM), key_gain.reshape(HEADS, HEAD_DIM), cot)
    part = width // PARTS

    def columns(rows):
        return pl.BlockSpec((rows, part), lambda i: (0, i))

    grad, patch_out, gq, gk = pl.pallas_call(
        finish,
        grid=(PARTS,),
        out_shape=(shape((128, width), f32), shape((PIECE, width), bf16),
                   shape((HEADS, HEAD_DIM), f32), shape((HEADS, HEAD_DIM), f32)),
        in_specs=[VMEM, VMEM, columns(PIECE), columns(1), VMEM, columns(PIECE), VMEM],
        out_specs=(columns(128), columns(PIECE), VMEM, VMEM),
        compiler_params=pltpu.CompilerParams(vmem_limit_bytes=62 << 20),
    )(patch_starts, patch_lengths, dpool, spill_back, inverse_before, out_rows, plane)
    return patch_out[None], grad[None], gq.reshape(width), gk.reshape(width)


def solution(mesh):
    rows = P("dp", "seq", None)
    flat = P("dp", "seq")
    return jax.shard_map(
        on_device,
        mesh=mesh,
        in_specs=(rows, flat, flat, P(), P(), rows),
        out_specs=(rows, rows, P(), P()),
        check_vma=False,
    )
```

```python
import functools
import math

import jax
import jax.numpy as jnp
from jax import lax
from jax.experimental import pallas as pl
from jax.experimental.pallas import tpu as pltpu
from jax.sharding import PartitionSpec as P

f32 = jnp.float32
bf16 = jnp.bfloat16
HEAD_DIM = 128
HEADS = 32
PIECE = 32
BLOCK = 512
EPS = 1e-6
NT = (((1,), (1,)), ((), ()))
TN = (((0,), (0,)), ((), ()))


def place():
    seq = lax.axis_index("seq")
    core = lax.axis_index("dp")
    y = seq // 32
    return seq, core, y, (seq // 8) % 4, seq % 8


def at(seq, core):
    return {"seq": seq, "dp": core}


def low_block(y, core):
    return core + 2 * (((y + 1) // 2) % 2)


def owner(y, x, doc):
    block = 2 * y + x // 2
    high = block // 4
    low = block + high * (7 - 2 * block)
    half = low // 2
    return (doc * (3 - half) + (1 - doc) * half), low % 2, high


def source(y, core, i):
    low = low_block(y, core)
    high = i // 16
    block = low + high * (7 - 2 * low)
    return block * 16 + i % 16, y // 2, i * PIECE


def head_at(x, z, i):
    return ((x + i // 8) % 4) * 8 + (z + i % 8) % 8


MESH = pl.DeviceIdType.MESH


def signal(sem, seq, core):
    pl.semaphore_signal(sem, inc=1, device_id=at(seq, core), device_id_type=MESH)


def remote(src, dst, send, recv, seq, core):
    return pltpu.make_async_remote_copy(
        src_ref=src, dst_ref=dst, send_sem=send, recv_sem=recv,
        device_id=at(seq, core), device_id_type=MESH,
    )


def column(row, count):
    r = lax.broadcasted_iota(jnp.int32, (count, count), 0)
    c = lax.broadcasted_iota(jnp.int32, (count, count), 1)
    return jnp.sum(jnp.where(r == c, jnp.broadcast_to(row, (count, count)), 0), 1, keepdims=True)


SCALE = HEAD_DIM ** -0.5
C2 = SCALE * math.log2(math.e)
STEPS = 9
GROUP = BLOCK // HEAD_DIM


def chunk(j):
    return pl.ds(pl.multiple_of(j * BLOCK, BLOCK), BLOCK)


def lanes(x, op):
    parts = [x[:, g * HEAD_DIM:(g + 1) * HEAD_DIM] for g in range(x.shape[1] // HEAD_DIM)]
    return functools.reduce(op, parts)


def step_at(low, t):
    if isinstance(t, int) and t in (0, 7, 8):
        return {0: (0, low), 7: (1, low), 8: (1, 7 - low)}[t]
    mask = 3 - (t - 1) // 2
    second = (t - 1) % 2
    odd, far = mask % 2, mask // 2
    chunk_low = (low + odd) % 2 + 2 * ((low // 2 + far) % 2)
    mirrored = second * (far * (1 - low // 2) + (1 - far) * (1 - low % 2))
    return 1 - second + mirrored, chunk_low + mirrored * (7 - 2 * chunk_low)


def over_steps(body, between=None):
    body((0, 8, 7))
    if between is not None:
        between()

    def three(i, _):
        body(tuple(1 + 3 * i + u for u in range(3)))
        return 0

    lax.fori_loop(0, 2, three, 0)


def tiled(x):
    return jnp.concatenate([x] * GROUP, 1)


def forward(low, values, keyed, query, s_ref, w_ref, stat, mixed, between):
    stat[...] = jnp.full(stat.shape, -1e30, f32)

    def cols(t):
        return pl.ds(pl.multiple_of(t * BLOCK, BLOCK), BLOCK)

    def scores(steps):
        for t in steps:
            high, j = step_at(low, t)
            s = lax.dot_general(query[chunk(high), :], keyed[chunk(j), :], NT, preferred_element_type=f32)
            if isinstance(t, int) and t != 7:
                r = lax.broadcasted_iota(jnp.int32, s.shape, 0)
                c = lax.broadcasted_iota(jnp.int32, s.shape, 1)
                s = jnp.where(c <= r, s, -1e30)
            s_ref[:, cols(t)] = s
            stat[chunk(high), :] = jnp.maximum(stat[chunk(high), :], lanes(s, jnp.maximum))

    over_steps(scores, between)
    stat[...] = jnp.broadcast_to(jnp.max(stat[...], -1, keepdims=True), stat.shape)
    mixed[...] = jnp.zeros(mixed.shape, f32)

    def expo(steps):
        for t in steps:
            high, j = step_at(low, t)
            e = jnp.exp2((s_ref[:, cols(t)] - tiled(stat[chunk(high), :])) * C2)
            s_ref[:, cols(t)] = e
            mixed[chunk(high), :] += lanes(e, jnp.add)

    over_steps(expo)
    stat[...] = jnp.broadcast_to(1.0 / jnp.sum(mixed[...], -1, keepdims=True), stat.shape)
    mixed[...] = jnp.zeros(mixed.shape, f32)

    def mix(steps):
        for t in steps:
            high, j = step_at(low, t)
            w = (s_ref[:, cols(t)] * tiled(stat[chunk(high), :])).astype(bf16)
            w_ref[:, cols(t)] = w
            mixed[chunk(high), :] += jnp.dot(w, values(j), preferred_element_type=f32)

    over_steps(mix)


def normed(mixed, out):
    m = mixed[...]
    rs = 1.0 / jnp.sqrt(jnp.mean(m * m, -1, keepdims=True) + EPS)
    out[...] = (m * rs).astype(bf16)
    return rs


def backward(low, values, keyed, query, dmb, s_ref, w_ref, d_ref, stat, delta, dk, dv, dq, after):
    def cols(t):
        return pl.ds(pl.multiple_of(t * BLOCK, BLOCK), BLOCK)

    def dvalue(t, high, j):
        dv[chunk(j), :] += lax.dot_general(w_ref[:, cols(t)], dmb[chunk(high), :], TN, preferred_element_type=f32)

    delta[...] = jnp.zeros(delta.shape, f32)

    def dprobs(steps, far):
        for t in steps:
            high, j = step_at(low, t)
            dp = lax.dot_general(dmb[chunk(high), :], values(j), NT, preferred_element_type=f32)
            d_ref[:, cols(t)] = dp
            delta[chunk(high), :] += lanes(dp * s_ref[:, cols(t)], jnp.add)
            if far:
                dvalue(t, high, j)

    dprobs((0, 8, 7), False)
    dprobs((5, 6), False)
    dprobs((1, 3), True)
    dprobs((2, 4), True)
    delta[...] = jnp.broadcast_to(jnp.sum(delta[...], -1, keepdims=True), delta.shape) * stat[...]
    stat[...] = stat[...] * SCALE
    dq[...] = jnp.zeros(dq.shape, f32)

    def dquery(ds, high, j):
        dq[chunk(high), :] += jnp.dot(ds, keyed[chunk(j), :], preferred_element_type=f32)

    def back(steps, far):
        for t in steps:
            high, j = step_at(low, t)
            ds = ((s_ref[:, cols(t)] * tiled(stat[chunk(high), :]))
                  * (d_ref[:, cols(t)] - tiled(delta[chunk(high), :]))).astype(bf16)
            if not far:
                dvalue(t, high, j)
            dk[chunk(j), :] += lax.dot_general(ds, query[chunk(high), :], TN, preferred_element_type=f32)
            if far:
                w_ref[:, cols(t)] = ds
            else:
                dquery(ds, high, j)

    back((1, 3), True)
    after(0)
    back((2, 4), True)
    after(1)
    back((5, 6), False)
    after(2)
    for t in (1, 2, 3, 4):
        dquery(w_ref[:, cols(t)], *step_at(low, t))
    back((0, 8, 7), False)
    after(3)


def whole(states, starts, lengths, qgain_all, kgain_all, cot_rows,
          patch_out, dpool, spill_back, plane, inverse_before,
          bytes_in, cot_in, cot, pooled, sums, spill, spill_in, inverse_out, kfull, cot_h, out_h,
          keyed, query, s_ref, w_ref, d_ref, dk, dv, dq, stat, delta, mixed, dmb,
          from_sib, to_far, from_far, mine_b, last_rows, column_in,
          s_load, s_spill, r_spill, s_pool, r_pool, s_cot, r_cot, s_key, r_key,
          s_out, r_out, s_sib, r_sib, s_far, r_far, s_dp, r_dp, s_col, r_col, s_pla, r_pla,
          s_last, r_last, s_inv, r_inv):
    seq, core, y, x, z = place()
    oy, ocore, ohigh = owner(y, x, core)
    mine = (oy == y) & (ocore == core)
    low = low_block(y, core)
    sib = low + 1 - 2 * (low % 2)
    far = low + 2 - 4 * (low // 2)
    farsib = sib + 2 - 4 * (sib // 2)
    partner = seq + 32 - 64 * (y % 2)
    before = (seq + 127) % 128
    after = (seq + 1) % 128
    head = x * 8 + z
    by, bcore, _high = owner(before // 32, (before // 8) % 4, core)
    mine_before = (by == y) & (bcore == core)
    pending = []

    def wait_all(ref, sem):
        pltpu.make_async_copy(ref, ref, sem).wait()

    def sent(ref, part, sem, own=mine):
        @pl.when(own)
        def _():
            wait_all(part, sem)

        @pl.when(jnp.logical_not(own))
        def _():
            wait_all(ref, sem)

    load_bytes = pltpu.make_async_copy(states, bytes_in, s_load.at[0])
    load_cot = pltpu.make_async_copy(cot_rows, cot_in, s_load.at[1])
    load_bytes.start()
    load_cot.start()

    barrier = pltpu.get_barrier_semaphore()
    signal(barrier, before, core)
    signal(barrier, after, core)

    def greet(i, _):
        s, d, _row = source(y, core, (i + head) % 32)

        @pl.when((s != seq) | (d != core))
        def _():
            signal(barrier, s, d)

        return 0

    lax.fori_loop(0, 32, greet, 0)

    def greet_column(i, _):
        c = (y * 2 + core + i) % 8
        signal(barrier, (c // 2) * 32 + head, c % 2)
        return 0

    lax.fori_loop(1, 8, greet_column, 0)

    base = seq * 128
    start = column(starts[...], PIECE) - base
    length = column(lengths[...], PIECE)
    at_byte = lax.broadcasted_iota(jnp.int32, (PIECE, 128), 1)
    member = ((at_byte >= start) & (at_byte < start + length)).astype(f32).astype(bf16)
    first = starts[:, 0:1] - base
    lead = (lax.broadcasted_iota(jnp.int32, (16, 128), 1) < first).astype(f32).astype(bf16)
    inverse = 1.0 / length.astype(f32)
    inverse_out[...] = jnp.broadcast_to(inverse[PIECE - 1:PIECE, :], (1, HEAD_DIM))
    load_bytes.wait()
    spill[...] = jnp.dot(lead, bytes_in[...], preferred_element_type=f32)[0:1, :]
    sums[...] = jnp.dot(member, bytes_in[...], preferred_element_type=f32) * inverse

    @pl.when(mine)
    def _():
        pl.semaphore_wait(barrier, 31 + 7 + 2)

    @pl.when(jnp.logical_not(mine))
    def _():
        pl.semaphore_wait(barrier, 32 + 7 + 2)

    spilling = remote(spill, spill_in, s_spill, r_spill, before, core)
    spilling.start()
    telling = remote(inverse_out, inverse_before, s_inv, r_inv, after, core)
    telling.start()
    pending.extend([spilling.wait_send, telling.wait])

    def scatter_rows(src, dst, first_row, count, send, recv):
        def step(i, _):
            h = head_at(x, z, i)
            part = src.at[h, pl.ds(first_row, count), :]
            target = oy * 32 + h
            local = (target == seq) & (ocore == core)

            @pl.when(local)
            def _():
                pltpu.make_async_copy(part, dst, recv).start()

            @pl.when(jnp.logical_not(local))
            def _():
                remote(part, dst, send, recv, target, ocore).start()

            return 0

        lax.fori_loop(0, 32, step, 0)

    def by_head(ref, first_row, value):
        for h in range(HEADS):
            ref[h, first_row:first_row + value.shape[0], :] = value[:, h * HEAD_DIM:(h + 1) * HEAD_DIM]

    by_head(pooled, 0, sums[0:16, :].astype(bf16))
    scatter_rows(pooled, kfull.at[seq, pl.ds(0, 16), :], 0, 16, s_pool.at[0], r_pool.at[0])
    spilling.wait_recv()
    last = (lax.broadcasted_iota(jnp.int32, (16, 1), 0) == 15) & (seq < 127)
    by_head(pooled, 16, (sums[16:32, :] + jnp.where(last, spill_in[...] * inverse[16:32, :], 0.0)).astype(bf16))
    scatter_rows(pooled, kfull.at[seq, pl.ds(16, 16), :], 16, 16, s_pool.at[1], r_pool.at[1])
    for i in range(2):
        half = pl.ds(16 * i, 16)
        pending.append(functools.partial(sent, pooled.at[:, half, :], pooled.at[0:31, half, :], s_pool.at[i]))

    qgain = qgain_all[pl.ds(head, 1), :]
    kgain = kgain_all[pl.ds(head, 1), :]

    def clear(j, _):
        dk[chunk(j), :] = jnp.zeros((BLOCK, HEAD_DIM), f32)
        dv[chunk(j), :] = jnp.zeros((BLOCK, HEAD_DIM), f32)
        return 0

    lax.fori_loop(0, 8, clear, 0)
    load_cot.wait()
    by_head(cot, 0, cot_in[...])
    crow = pl.multiple_of(ohigh * BLOCK + (seq % 16) * PIECE, PIECE)

    def pieces(block):
        return pl.ds(block * 16, 16)

    def values(block):
        return kfull[pieces(block)].reshape(BLOCK, HEAD_DIM)

    def prepare(block):
        keyed[chunk(block), :] = (values(block).astype(f32) * kgain).astype(bf16)

    across, beside, relays = {}, {}, {}
    for half in range(2):
        rows = pl.ds(16 * half, 16)
        wait_all(kfull.at[pl.ds(0, 32), rows, :], r_pool.at[half])
        for i, block in enumerate((low, 7 - low)):
            n = 2 * half + i
            there = kfull.at[pieces(block), rows, :]
            across[n] = remote(there, there, s_key.at[n], r_key.at[n], partner, core)
            across[n].start()
            beside[n] = remote(there, there, s_key.at[4 + n], r_key.at[4 + n], seq, 1 - core)
            beside[n].start()
            pending.extend([across[n].wait_send, beside[n].wait_send])
    scatter_rows(cot, cot_h.at[pl.ds(crow, PIECE), :], 0, PIECE, s_cot, r_cot)
    pending.append(functools.partial(sent, cot, cot.at[0:31], s_cot))
    for i, block in enumerate((low, 7 - low)):
        query[chunk(i), :] = (values(block).astype(f32) * qgain).astype(bf16)
        prepare(block)

    def other_keys():
        for n in range(4):
            block = (far, 7 - far)[n % 2]
            across[n].wait_recv()
            there = kfull.at[pieces(block), pl.ds(16 * (n // 2), 16), :]
            relays[n] = remote(there, there, s_key.at[8 + n], r_key.at[8 + n], seq, 1 - core)
            relays[n].start()
            pending.append(relays[n].wait_send)
            beside[n].wait_recv()
        for block in (sib, 7 - sib, far, 7 - far):
            prepare(block)
        for n in range(4):
            relays[n].wait_recv()
        for block in (farsib, 7 - farsib):
            prepare(block)

    forward(low, values, keyed, query, s_ref, w_ref, stat, mixed, other_keys)
    rs = normed(mixed, out_h)

    head_columns = pl.ds(pl.multiple_of(head * HEAD_DIM, HEAD_DIM), HEAD_DIM)

    def scatter_back(first, count, part_of, there, send, recv, shift=0):
        def step(i, _):
            n = first + (i + head) % count
            s, d, row = source(y, core, n)
            s = (s + shift) % 128
            part = part_of(n)
            local = (s == seq) & (d == core)

            @pl.when(local)
            def _():
                pltpu.make_async_copy(part, there, recv).start()

            @pl.when(jnp.logical_not(local))
            def _():
                remote(part, there, send, recv, s, d).start()

            return 0

        lax.fori_loop(0, count, step, 0)

    def rows_of(ref):
        return lambda n: ref.at[pl.ds(pl.multiple_of(n * PIECE, PIECE), PIECE), :]

    scatter_back(0, 32, rows_of(out_h), patch_out.at[head], s_out, r_out)
    pending.append(functools.partial(sent, out_h, out_h.at[0:31 * PIECE], s_out))
    pending.append(functools.partial(wait_all, patch_out, r_out))
    wait_all(cot_h, r_cot)
    g = cot_h[...].astype(f32)
    m = mixed[...]
    dmb[...] = (g * rs - m * (jnp.sum(g * m, -1, keepdims=True) * (rs * rs * rs) * (1.0 / HEAD_DIM))).astype(bf16)

    gk = [jnp.zeros((1, HEAD_DIM), f32)]
    to_sib, to_partner = [], []

    def complete(block):
        d = dk[chunk(block), :]
        dv[chunk(block), :] += d * kgain
        gk[0] = gk[0] + jnp.sum(d * values(block).astype(f32), 0, keepdims=True)

    def give_sib(block):
        i = len(to_sib)
        to_sib.append(remote(dv.at[chunk(block), :], from_sib.at[i], s_sib.at[i], r_sib.at[i], seq, 1 - core))
        to_sib[i].start()
        pending.append(to_sib[i].wait_send)

    outer = 1 - low // 2

    def in_turn(block, turn):
        return block + ((turn + outer + 1) % 2) * (7 - 2 * block)

    def combine(turn):
        to_sib[turn].wait_recv()
        to_far[turn] = (dv[chunk(in_turn(far, turn)), :] + from_sib[turn]).astype(bf16)
        to_partner.append(remote(to_far.at[turn], from_far.at[turn], s_far.at[turn], r_far.at[turn], partner, core))
        to_partner[turn].start()
        pending.append(to_partner[turn].wait_send)

    def after_steps(n):
        if n < 2:
            complete(in_turn(farsib, n))
            give_sib(in_turn(farsib, n))
            complete(in_turn(far, n))
        else:
            for block in ((sib, 7 - sib), (low, 7 - low))[n - 2]:
                complete(block)
                if n == 2:
                    give_sib(block)
        if n in (1, 2):
            combine(n - 1)

    backward(low, values, keyed, query, dmb, s_ref, w_ref, d_ref, stat, delta, dk, dv, dq, after_steps)
    gq = jnp.zeros((1, HEAD_DIM), f32)
    for i, block in enumerate((low, 7 - low)):
        gq = gq + jnp.sum(dq[chunk(i), :] * values(block).astype(f32), 0, keepdims=True)
    place_in_column = pl.ds(y * 2 + core, 1)
    column_in[place_in_column] = jnp.concatenate([gq, gk[0]], 0)[None]

    def send_column(i, _):
        c = (y * 2 + core + i) % 8
        slot = column_in.at[place_in_column]
        remote(slot, slot, s_col, r_col, (c // 2) * 32 + head, c % 2).start()
        return 0

    lax.fori_loop(1, 8, send_column, 0)
    to_sib[2].wait_recv()
    to_sib[3].wait_recv()
    for turn in range(2):
        high = (turn + outer) % 2
        mixed[chunk(high), :] = (dv[chunk(low + high * (7 - 2 * low)), :] + from_sib[2 + high]
                                 + dq[chunk(high), :] * qgain)
        to_partner[turn].wait_recv()
        mixed[chunk(high), :] += from_far[turn].astype(f32)
        mine_b[chunk(high), :] = mixed[chunk(high), :].astype(bf16)
        scatter_back(16 * high, 16, rows_of(mine_b), dpool.at[head], s_dp, r_dp)
        for i in range(16):
            last_rows[16 * high + i] = mixed[pl.ds(high * BLOCK + i * PIECE + PIECE - 1, 1), :]
        scatter_back(16 * high, 16, lambda n: last_rows.at[n], spill_back.at[:, head_columns], s_last, r_last, 1)
        if turn == 0:
            wait_all(column_in.at[0:7], r_col)
            total = column_in[0]
            for i in range(1, 8):
                total = total + column_in[i]
            wait_all(column_in.at[0:7], s_col)
            column_in[place_in_column] = total[None]
            scatter_back(0, 32, lambda n: column_in.at[y * 2 + core], plane.at[head], s_pla, r_pla)
    pending.append(functools.partial(sent, mine_b, mine_b.at[0:31 * PIECE], s_dp))
    pending.append(functools.partial(sent, last_rows, last_rows.at[0:31], s_last, mine_before))
    pending.append(functools.partial(sent, plane, plane.at[0:31], s_pla))
    wait_all(dpool, r_dp)
    wait_all(spill_back, r_last)
    wait_all(plane, r_pla)
    for wait in pending:
        wait()


def finish(starts, lengths, dpool, spill_back, inverse_before, out_in, plane, grad, patch_out, gq, gk,
           starts_v, lengths_v, dpool_v, spill_v, inverse_v, out_v, plane_v, grad_v, rows_v, gains_v, s_in, s_to):
    loads = []
    for n, (src, dst) in enumerate(((starts, starts_v), (lengths, lengths_v), (spill_back, spill_v),
                                    (inverse_before, inverse_v), (out_in, out_v), (plane, plane_v))):
        loads.append(pltpu.make_async_copy(src, dst, s_in.at[n]))
    each = HEADS // PARTS
    parts = []
    for p in range(PARTS):
        heads = pl.ds(p * each, each)
        parts.append(pltpu.make_async_copy(dpool.at[heads], dpool_v.at[heads], s_in.at[len(loads) + p]))
    for copy in loads[:4] + parts + loads[4:]:
        copy.start()
    for copy in loads[:4]:
        copy.wait()
    base = lax.axis_index("seq") * 128
    start = starts_v[...] - base
    length = lengths_v[...]
    at_byte = lax.broadcasted_iota(jnp.int32, (128, PIECE), 0)
    inside = (at_byte >= start) & (at_byte < start + length)
    member = inside.astype(f32).astype(bf16)
    by_byte = jnp.sum(jnp.where(inside, 1.0 / length.astype(f32), 0.0), 1, keepdims=True)
    lead = lax.broadcasted_iota(jnp.int32, (8, 1), 0) < start[:, 0:1]
    stores = []

    def store(src, dst):
        stores.append(pltpu.make_async_copy(src, dst, s_to.at[len(stores)]))
        stores[-1].start()

    for p in range(PARTS):
        parts[p].wait()
        for h in range(p * each, (p + 1) * each):
            columns = slice(h * HEAD_DIM, (h + 1) * HEAD_DIM)
            grad_v[:, columns] = jnp.dot(member, dpool_v[h], preferred_element_type=f32) * by_byte
            grad_v[0:8, columns] = jnp.where(lead, spill_v[:, columns] * inverse_v[...], grad_v[0:8, columns])
        columns = pl.ds(p * each * HEAD_DIM, each * HEAD_DIM)
        store(grad_v.at[:, columns], grad.at[:, columns])
    loads[4].wait()
    for h in range(HEADS):
        rows_v[:, h * HEAD_DIM:(h + 1) * HEAD_DIM] = out_v[h]
    store(rows_v, patch_out)
    loads[5].wait()
    for h in range(HEADS):
        for i in range(2):
            gains_v[i, h:h + 1, :] = plane_v[h, i:i + 1, :]
    store(gains_v.at[0], gq)
    store(gains_v.at[1], gk)
    for copy in stores:
        copy.wait()


VMEM = pl.BlockSpec(memory_space=pltpu.VMEM)
ANY = pl.BlockSpec(memory_space=pl.ANY)
DMA = pltpu.SemaphoreType.DMA
PARTS = 4


def shape(dims, dtype):
    return jax.ShapeDtypeStruct(dims, dtype)


def on_device(byte_states, patch_starts, patch_lengths, query_gain, key_gain, out_cotangent):
    states = byte_states[0]
    cot = out_cotangent[0]
    width = states.shape[1]
    own = 2 * BLOCK
    keys = 8 * BLOCK
    by_head = (HEADS, PIECE, HEAD_DIM)
    V = pltpu.VMEM
    out_rows, dpool, spill_back, plane, inverse_before = pl.pallas_call(
        whole,
        out_shape=(shape(by_head, bf16), shape(by_head, bf16), shape((1, width), f32),
                   shape((HEADS, 2, HEAD_DIM), f32), shape((1, HEAD_DIM), f32)),
        in_specs=[ANY, VMEM, VMEM, VMEM, VMEM, ANY],
        out_specs=(ANY,) * 5,
        scratch_shapes=[
            V((128, width), bf16), V((PIECE, width), bf16), V(by_head, bf16), V(by_head, bf16), V((PIECE, width), f32),
            V((1, width), f32), V((1, width), f32), V((1, HEAD_DIM), f32),
            V((128, PIECE, HEAD_DIM), bf16), V((own, HEAD_DIM), bf16), V((own, HEAD_DIM), bf16),
            V((keys, HEAD_DIM), bf16), V((own, HEAD_DIM), bf16),
            V((BLOCK, STEPS * BLOCK), f32), V((BLOCK, STEPS * BLOCK), bf16), V((BLOCK, STEPS * BLOCK), f32),
            V((keys, HEAD_DIM), f32), V((keys, HEAD_DIM), f32),
            V((own, HEAD_DIM), f32), V((own, HEAD_DIM), f32), V((own, HEAD_DIM), f32), V((own, HEAD_DIM), f32),
            V((own, HEAD_DIM), bf16),
            V((4, BLOCK, HEAD_DIM), f32), V((2, BLOCK, HEAD_DIM), bf16), V((2, BLOCK, HEAD_DIM), bf16),
            V((own, HEAD_DIM), bf16), V((HEADS, 1, HEAD_DIM), f32), V((8, 2, HEAD_DIM), f32),
            DMA((2,)), DMA, DMA, DMA((2,)), DMA((2,)), DMA, DMA, DMA((12,)), DMA((12,)),
            DMA, DMA, DMA((4,)), DMA((4,)), DMA((2,)), DMA((2,)), DMA, DMA, DMA, DMA, DMA, DMA,
            DMA, DMA, DMA, DMA,
        ],
        compiler_params=pltpu.CompilerParams(
            collective_id=0, has_side_effects=True, vmem_limit_bytes=56 << 20
        ),
    )(states, patch_starts, patch_lengths, query_gain.reshape(HEADS, HEAD_DIM), key_gain.reshape(HEADS, HEAD_DIM), cot)
    grad, patch_out, gq, gk = pl.pallas_call(
        finish,
        out_shape=(shape((128, width), f32), shape((PIECE, width), bf16),
                   shape((HEADS, HEAD_DIM), f32), shape((HEADS, HEAD_DIM), f32)),
        in_specs=[ANY] * 7,
        out_specs=(ANY,) * 4,
        scratch_shapes=[
            V((1, PIECE), jnp.int32), V((1, PIECE), jnp.int32), V(by_head, bf16), V((1, width), f32),
            V((1, HEAD_DIM), f32), V(by_head, bf16), V((HEADS, 2, HEAD_DIM), f32), V((128, width), f32),
            V((PIECE, width), bf16), V((2, HEADS, HEAD_DIM), f32), DMA((6 + PARTS,)), DMA((3 + PARTS,)),
        ],
        compiler_params=pltpu.CompilerParams(vmem_limit_bytes=62 << 20),
    )(patch_starts, patch_lengths, dpool, spill_back, inverse_before, out_rows, plane)
    return patch_out[None], grad[None], gq.reshape(width), gk.reshape(width)


def solution(mesh):
    rows = P("dp", "seq", None)
    flat = P("dp", "seq")
    return jax.shard_map(
        on_device,
        mesh=mesh,
        in_specs=(rows, flat, flat, P(), P(), rows),
        out_specs=(rows, rows, P(), P()),
        check_vma=False,
    )
```

```python
import functools
import math

import jax
import jax.numpy as jnp
from jax import lax
from jax.experimental import pallas as pl
from jax.experimental.pallas import tpu as pltpu
from jax.sharding import PartitionSpec as P

f32 = jnp.float32
bf16 = jnp.bfloat16
HEAD_DIM = 128
HEADS = 32
PIECE = 32
BLOCK = 512
EPS = 1e-6
NT = (((1,), (1,)), ((), ()))
TN = (((0,), (0,)), ((), ()))


def place():
    seq = lax.axis_index("seq")
    core = lax.axis_index("dp")
    y = seq // 32
    return seq, core, y, (seq // 8) % 4, seq % 8


def at(seq, core):
    return {"seq": seq, "dp": core}


def low_block(y, core):
    return core + 2 * (((y + 1) // 2) % 2)


def owner(y, x, doc):
    block = 2 * y + x // 2
    high = block // 4
    low = block + high * (7 - 2 * block)
    half = low // 2
    return (doc * (3 - half) + (1 - doc) * half), low % 2, high


def source(y, core, i):
    low = low_block(y, core)
    high = i // 16
    block = low + high * (7 - 2 * low)
    return block * 16 + i % 16, y // 2, i * PIECE


def head_at(x, z, i):
    return ((x + i // 8) % 4) * 8 + (z + i % 8) % 8


MESH = pl.DeviceIdType.MESH


def signal(sem, seq, core):
    pl.semaphore_signal(sem, inc=1, device_id=at(seq, core), device_id_type=MESH)


def remote(src, dst, send, recv, seq, core):
    return pltpu.make_async_remote_copy(
        src_ref=src, dst_ref=dst, send_sem=send, recv_sem=recv,
        device_id=at(seq, core), device_id_type=MESH,
    )


def column(row, count):
    r = lax.broadcasted_iota(jnp.int32, (count, count), 0)
    c = lax.broadcasted_iota(jnp.int32, (count, count), 1)
    return jnp.sum(jnp.where(r == c, jnp.broadcast_to(row, (count, count)), 0), 1, keepdims=True)


SCALE = HEAD_DIM ** -0.5
C2 = SCALE * math.log2(math.e)
STEPS = 9
GROUP = BLOCK // HEAD_DIM


def chunk(j):
    return pl.ds(pl.multiple_of(j * BLOCK, BLOCK), BLOCK)


def lanes(x, op):
    parts = [x[:, g * HEAD_DIM:(g + 1) * HEAD_DIM] for g in range(x.shape[1] // HEAD_DIM)]
    return functools.reduce(op, parts)


def step_at(low, t):
    if isinstance(t, int) and t in (0, 7, 8):
        return {0: (0, low), 7: (1, low), 8: (1, 7 - low)}[t]
    mask = 3 - (t - 1) // 2
    second = (t - 1) % 2
    odd, far = mask % 2, mask // 2
    chunk_low = (low + odd) % 2 + 2 * ((low // 2 + far) % 2)
    mirrored = second * (far * (1 - low // 2) + (1 - far) * (1 - low % 2))
    return 1 - second + mirrored, chunk_low + mirrored * (7 - 2 * chunk_low)


def group(t):
    return 1 if t in (1, 2, 3, 4) else 0


def tiled(x):
    return jnp.concatenate([x] * GROUP, 1)


def forward(low, values, keyed, query, s_ref, w_ref, stat, delta, mixed, early, sib_keys, far_keys, farsib_keys):
    def cols(t):
        return pl.ds(t * BLOCK, BLOCK)

    stat[...] = jnp.full(stat.shape, -1e30, f32)
    delta[...] = jnp.zeros(delta.shape, f32)
    mixed[...] = jnp.zeros(mixed.shape, f32)

    def scores(steps):
        for t in steps:
            high, j = step_at(low, t)
            s = lax.dot_general(query[chunk(high), :], keyed[chunk(j), :], NT, preferred_element_type=f32)
            if t in (0, 8):
                r = lax.broadcasted_iota(jnp.int32, s.shape, 0)
                c = lax.broadcasted_iota(jnp.int32, s.shape, 1)
                s = jnp.where(c <= r, s, -1e30)
            s_ref[:, cols(t)] = s
            here = stat.at[group(t), chunk(high), :]
            here[...] = jnp.maximum(here[...], lanes(s, jnp.maximum))

    def expo(steps):
        g = group(steps[0])
        stat[g] = jnp.broadcast_to(jnp.max(stat[g], -1, keepdims=True), stat.shape[1:])
        for t in steps:
            high, j = step_at(low, t)
            e = jnp.exp2((s_ref[:, cols(t)] - tiled(stat[g, chunk(high), :])) * C2)
            s_ref[:, cols(t)] = e
            delta[g, chunk(high), :] += lanes(e, jnp.add)

    scores((0, 8, 7))
    early()
    sib_keys()
    scores((5, 6))
    expo((0, 8, 7, 5, 6))
    far_keys()
    scores((3, 4))
    farsib_keys()
    scores((1, 2))
    expo((3, 4, 1, 2))
    top = jnp.maximum(stat[0], stat[1])
    parts = [jnp.exp2((stat[g] - top) * C2) for g in range(2)]
    total = sum(parts[g] * jnp.sum(delta[g], -1, keepdims=True) for g in range(2))
    for g in range(2):
        stat[g] = parts[g] / total

    def mix(steps):
        for t in steps:
            high, j = step_at(low, t)
            w = (s_ref[:, cols(t)] * tiled(stat[group(t), chunk(high), :])).astype(bf16)
            w_ref[:, cols(t)] = w
            mixed[chunk(high), :] += jnp.dot(w, values(j), preferred_element_type=f32)

    for steps in ((0, 8, 7), (5, 6, 3), (4, 1, 2)):
        mix(steps)


def normed(mixed, out):
    m = mixed[...]
    rs = 1.0 / jnp.sqrt(jnp.mean(m * m, -1, keepdims=True) + EPS)
    out[...] = (m * rs).astype(bf16)
    return rs


def backward(low, values, keyed, query, dmb, s_ref, w_ref, d_ref, stat, delta, dk, dv, dq, after):
    def cols(t):
        return pl.ds(t * BLOCK, BLOCK)

    def dvalue(t, high, j):
        dv[chunk(j), :] += lax.dot_general(w_ref[:, cols(t)], dmb[chunk(high), :], TN, preferred_element_type=f32)

    delta[...] = jnp.zeros(delta.shape, f32)

    def dprobs(steps):
        for t in steps:
            high, j = step_at(low, t)
            dp = lax.dot_general(dmb[chunk(high), :], values(j), NT, preferred_element_type=f32)
            d_ref[:, cols(t)] = dp
            delta[group(t), chunk(high), :] += lanes(dp * s_ref[:, cols(t)], jnp.add)

    for steps in ((0, 8, 7), (5, 6, 3), (4, 1, 2)):
        dprobs(steps)
    summed = sum(jnp.sum(delta[g], -1, keepdims=True) * stat[g] for g in range(2))
    delta[0] = summed
    stat[...] = stat[...] * SCALE
    dq[...] = jnp.zeros(dq.shape, f32)

    def dquery(ds, high, j):
        dq[chunk(high), :] += jnp.dot(ds, keyed[chunk(j), :], preferred_element_type=f32)

    def back(steps, far):
        for t in steps:
            high, j = step_at(low, t)
            ds = ((s_ref[:, cols(t)] * tiled(stat[group(t), chunk(high), :]))
                  * (d_ref[:, cols(t)] - tiled(delta[0, chunk(high), :]))).astype(bf16)
            dvalue(t, high, j)
            dk[chunk(j), :] += lax.dot_general(ds, query[chunk(high), :], TN, preferred_element_type=f32)
            if far:
                w_ref[:, cols(t)] = ds
            else:
                dquery(ds, high, j)

    back((1, 3), True)
    after(0)
    back((2, 4), True)
    after(1)
    back((5, 6), False)
    after(2)
    for t in (1, 2, 3, 4):
        dquery(w_ref[:, cols(t)], *step_at(low, t))
    back((0, 8, 7), False)
    after(3)


def whole(states, starts, lengths, qgain_all, kgain_all, cot_rows,
          patch_out, dpool, spill_back, plane, inverse_before,
          bytes_in, cot_in, cot, pooled, sums, spill, spill_in, inverse_out, kfull, cot_h, out_h,
          keyed, query, s_ref, w_ref, d_ref, dk, dv, dq, stat, delta, mixed, dmb,
          from_sib, to_far, from_far, mine_b, last_rows, column_in, gains,
          s_load, s_spill, r_spill, s_pool, r_pool, s_cot, r_cot, s_key, r_key,
          s_out, r_out, s_sib, r_sib, s_far, r_far, s_dp, r_dp, s_col, r_col, s_pla, r_pla,
          s_last, r_last, s_inv, r_inv):
    seq, core, y, x, z = place()
    oy, ocore, ohigh = owner(y, x, core)
    mine = (oy == y) & (ocore == core)
    low = low_block(y, core)
    sib = low + 1 - 2 * (low % 2)
    far = low + 2 - 4 * (low // 2)
    farsib = sib + 2 - 4 * (sib // 2)
    partner = seq + 32 - 64 * (y % 2)
    before = (seq + 127) % 128
    after = (seq + 1) % 128
    head = x * 8 + z
    by, bcore, _high = owner(before // 32, (before // 8) % 4, core)
    mine_before = (by == y) & (bcore == core)
    pending = []

    def wait_all(ref, sem):
        pltpu.make_async_copy(ref, ref, sem).wait()

    def sent(ref, part, sem, own=mine):
        @pl.when(own)
        def _():
            wait_all(part, sem)

        @pl.when(jnp.logical_not(own))
        def _():
            wait_all(ref, sem)

    load_bytes = pltpu.make_async_copy(states, bytes_in, s_load.at[0])
    load_cot = pltpu.make_async_copy(cot_rows, cot_in, s_load.at[1])
    load_bytes.start()
    load_cot.start()

    barrier = pltpu.get_barrier_semaphore()
    signal(barrier, before, core)
    signal(barrier, after, core)

    def greet(i, _):
        s, d, _row = source(y, core, (i + head) % 32)

        @pl.when((s != seq) | (d != core))
        def _():
            signal(barrier, s, d)

        return 0

    lax.fori_loop(0, 32, greet, 0)

    def greet_column(i, _):
        c = (y * 2 + core + i) % 8
        signal(barrier, (c // 2) * 32 + head, c % 2)
        return 0

    lax.fori_loop(1, 8, greet_column, 0)

    base = seq * 128
    start = column(starts[...], PIECE) - base
    length = column(lengths[...], PIECE)
    at_byte = lax.broadcasted_iota(jnp.int32, (PIECE, 128), 1)
    member = ((at_byte >= start) & (at_byte < start + length)).astype(f32).astype(bf16)
    first = starts[:, 0:1] - base
    lead = (lax.broadcasted_iota(jnp.int32, (16, 128), 1) < first).astype(f32).astype(bf16)
    inverse = 1.0 / length.astype(f32)
    inverse_out[...] = jnp.broadcast_to(inverse[PIECE - 1:PIECE, :], (1, HEAD_DIM))
    load_bytes.wait()
    spill[...] = jnp.dot(lead, bytes_in[...], preferred_element_type=f32)[0:1, :]
    sums[...] = jnp.dot(member, bytes_in[...], preferred_element_type=f32) * inverse

    @pl.when(mine)
    def _():
        pl.semaphore_wait(barrier, 31 + 7 + 2)

    @pl.when(jnp.logical_not(mine))
    def _():
        pl.semaphore_wait(barrier, 32 + 7 + 2)

    spilling = remote(spill, spill_in, s_spill, r_spill, before, core)
    spilling.start()
    telling = remote(inverse_out, inverse_before, s_inv, r_inv, after, core)
    telling.start()
    pending.extend([spilling.wait_send, telling.wait])

    def scatter_rows(src, dst, first_row, count, send, recv):
        def step(i, _):
            h = head_at(x, z, i)
            part = src.at[h, pl.ds(first_row, count), :]
            target = oy * 32 + h
            local = (target == seq) & (ocore == core)

            @pl.when(local)
            def _():
                pltpu.make_async_copy(part, dst, recv).start()

            @pl.when(jnp.logical_not(local))
            def _():
                remote(part, dst, send, recv, target, ocore).start()

            return 0

        lax.fori_loop(0, 32, step, 0)

    def by_head(ref, first_row, value):
        for h in range(HEADS):
            ref[h, first_row:first_row + value.shape[0], :] = value[:, h * HEAD_DIM:(h + 1) * HEAD_DIM]

    by_head(pooled, 0, sums[0:16, :].astype(bf16))
    scatter_rows(pooled, kfull.at[seq, pl.ds(0, 16), :], 0, 16, s_pool.at[0], r_pool.at[0])
    spilling.wait_recv()
    last = (lax.broadcasted_iota(jnp.int32, (16, 1), 0) == 15) & (seq < 127)
    by_head(pooled, 16, (sums[16:32, :] + jnp.where(last, spill_in[...] * inverse[16:32, :], 0.0)).astype(bf16))
    scatter_rows(pooled, kfull.at[seq, pl.ds(16, 16), :], 16, 16, s_pool.at[1], r_pool.at[1])
    for i in range(2):
        half = pl.ds(16 * i, 16)
        pending.append(functools.partial(sent, pooled.at[:, half, :], pooled.at[0:31, half, :], s_pool.at[i]))

    qgain = qgain_all[pl.ds(head, 1), :]
    kgain = kgain_all[pl.ds(head, 1), :]

    def clear(j, _):
        dk[chunk(j), :] = jnp.zeros((BLOCK, HEAD_DIM), f32)
        dv[chunk(j), :] = jnp.zeros((BLOCK, HEAD_DIM), f32)
        return 0

    lax.fori_loop(0, 8, clear, 0)
    load_cot.wait()
    by_head(cot, 0, cot_in[...])
    crow = pl.multiple_of(ohigh * BLOCK + (seq % 16) * PIECE, PIECE)

    def pieces(block):
        return pl.ds(block * 16, 16)

    def values(block):
        return kfull[pieces(block)].reshape(BLOCK, HEAD_DIM)

    def prepare(block):
        keyed[chunk(block), :] = (values(block).astype(f32) * kgain).astype(bf16)

    across, beside, relays = {}, {}, {}
    for half in range(2):
        rows = pl.ds(16 * half, 16)
        wait_all(kfull.at[pl.ds(0, 32), rows, :], r_pool.at[half])
        for i, block in enumerate((low, 7 - low)):
            n = 2 * half + i
            there = kfull.at[pieces(block), rows, :]
            across[n] = remote(there, there, s_key.at[n], r_key.at[n], partner, core)
            across[n].start()
            beside[n] = remote(there, there, s_key.at[4 + n], r_key.at[4 + n], seq, 1 - core)
            beside[n].start()
            pending.extend([across[n].wait_send, beside[n].wait_send])
    scatter_rows(cot, cot_h.at[pl.ds(crow, PIECE), :], 0, PIECE, s_cot, r_cot)
    pending.append(functools.partial(sent, cot, cot.at[0:31], s_cot))
    for i, block in enumerate((low, 7 - low)):
        query[chunk(i), :] = (values(block).astype(f32) * qgain).astype(bf16)
        prepare(block)

    def relay(n):
        across[n].wait_recv()
        there = kfull.at[pieces((far, 7 - far)[n % 2]), pl.ds(16 * (n // 2), 16), :]
        relays[n] = remote(there, there, s_key.at[8 + n], r_key.at[8 + n], seq, 1 - core)
        relays[n].start()
        pending.append(relays[n].wait_send)

    def early():
        relay(0)
        relay(1)

    def sib_keys():
        for n in range(4):
            beside[n].wait_recv()
        prepare(sib)
        prepare(7 - sib)

    def far_keys():
        relay(2)
        relay(3)
        prepare(far)
        prepare(7 - far)

    def farsib_keys():
        for n in range(4):
            relays[n].wait_recv()
        prepare(farsib)
        prepare(7 - farsib)

    forward(low, values, keyed, query, s_ref, w_ref, stat, delta, mixed, early, sib_keys, far_keys, farsib_keys)
    rs = normed(mixed, out_h)

    head_columns = pl.ds(pl.multiple_of(head * HEAD_DIM, HEAD_DIM), HEAD_DIM)

    def scatter_back(first, count, part_of, there, send, recv, shift=0):
        def step(i, _):
            n = first + (i + head) % count
            s, d, row = source(y, core, n)
            s = (s + shift) % 128
            part = part_of(n)
            local = (s == seq) & (d == core)

            @pl.when(local)
            def _():
                pltpu.make_async_copy(part, there, recv).start()

            @pl.when(jnp.logical_not(local))
            def _():
                remote(part, there, send, recv, s, d).start()

            return 0

        lax.fori_loop(0, count, step, 0)

    def rows_of(ref):
        return lambda n: ref.at[pl.ds(pl.multiple_of(n * PIECE, PIECE), PIECE), :]

    scatter_back(0, 32, rows_of(out_h), patch_out.at[head], s_out, r_out)
    pending.append(functools.partial(sent, out_h, out_h.at[0:31 * PIECE], s_out))
    pending.append(functools.partial(wait_all, patch_out, r_out))
    wait_all(cot_h, r_cot)
    g = cot_h[...].astype(f32)
    m = mixed[...]
    dmb[...] = (g * rs - m * (jnp.sum(g * m, -1, keepdims=True) * (rs * rs * rs) * (1.0 / HEAD_DIM))).astype(bf16)

    gk = [jnp.zeros((1, HEAD_DIM), f32)]
    to_sib, to_partner = [], []

    def complete(block):
        d = dk[chunk(block), :]
        dv[chunk(block), :] += d * kgain
        gk[0] = gk[0] + jnp.sum(d * values(block).astype(f32), 0, keepdims=True)

    def give_sib(block):
        i = len(to_sib)
        to_sib.append(remote(dv.at[chunk(block), :], from_sib.at[i], s_sib.at[i], r_sib.at[i], seq, 1 - core))
        to_sib[i].start()
        pending.append(to_sib[i].wait_send)

    outer = 1 - low // 2

    def in_turn(block, turn):
        return block + ((turn + outer + 1) % 2) * (7 - 2 * block)

    def combine(turn):
        to_sib[turn].wait_recv()
        to_far[turn] = (dv[chunk(in_turn(far, turn)), :] + from_sib[turn]).astype(bf16)
        to_partner.append(remote(to_far.at[turn], from_far.at[turn], s_far.at[turn], r_far.at[turn], partner, core))
        to_partner[turn].start()
        pending.append(to_partner[turn].wait_send)

    def after_steps(n):
        if n < 2:
            complete(in_turn(farsib, n))
            give_sib(in_turn(farsib, n))
            complete(in_turn(far, n))
        else:
            for block in ((sib, 7 - sib), (low, 7 - low))[n - 2]:
                complete(block)
                if n == 2:
                    give_sib(block)
        if n in (1, 2):
            combine(n - 1)

    backward(low, values, keyed, query, dmb, s_ref, w_ref, d_ref, stat, delta, dk, dv, dq, after_steps)
    gq = jnp.zeros((1, HEAD_DIM), f32)
    for i, block in enumerate((low, 7 - low)):
        gq = gq + jnp.sum(dq[chunk(i), :] * values(block).astype(f32), 0, keepdims=True)
    place_in_column = pl.ds(y * 2 + core, 1)
    column_in[place_in_column] = jnp.concatenate([gq, gk[0]], 0)[None]

    def send_column(i, _):
        c = (y * 2 + core + i) % 8
        slot = column_in.at[place_in_column]
        remote(slot, slot, s_col, r_col, (c // 2) * 32 + head, c % 2).start()
        return 0

    lax.fori_loop(1, 8, send_column, 0)
    to_sib[2].wait_recv()
    to_sib[3].wait_recv()
    for turn in range(2):
        high = (turn + outer) % 2
        mixed[chunk(high), :] = (dv[chunk(low + high * (7 - 2 * low)), :] + from_sib[2 + high]
                                 + dq[chunk(high), :] * qgain)
        to_partner[turn].wait_recv()
        mixed[chunk(high), :] += from_far[turn].astype(f32)
        mine_b[chunk(high), :] = mixed[chunk(high), :].astype(bf16)
        scatter_back(16 * high, 16, rows_of(mine_b), dpool.at[head], s_dp, r_dp)
        for i in range(16):
            last_rows[16 * high + i] = mixed[pl.ds(high * BLOCK + i * PIECE + PIECE - 1, 1), :]
        scatter_back(16 * high, 16, lambda n: last_rows.at[n], spill_back.at[:, head_columns], s_last, r_last, 1)
        if turn == 0:
            wait_all(column_in.at[0:7], r_col)
            total = column_in[0]
            for i in range(1, 8):
                total = total + column_in[i]
            gains[pl.ds(head, 1)] = total[None]

            def send_z(i, _):
                slot = gains.at[pl.ds(head, 1)]
                remote(slot, slot, s_pla.at[0], r_pla.at[0], y * 32 + x * 8 + (z + i) % 8, core).start()
                return 0

            lax.fori_loop(1, 8, send_z, 0)
    wait_all(gains.at[0:7], r_pla.at[0])

    def send_x(i, _):
        slots = gains.at[pl.ds(x * 8, 8)]
        remote(slots, slots, s_pla.at[1], r_pla.at[1], y * 32 + ((x + i) % 4) * 8 + z, core).start()
        return 0

    lax.fori_loop(1, 4, send_x, 0)
    pending.append(functools.partial(wait_all, column_in.at[0:7], s_col))
    pending.append(functools.partial(wait_all, gains.at[0:7], s_pla.at[0]))
    pending.append(functools.partial(wait_all, gains.at[0:24], s_pla.at[1]))
    pending.append(functools.partial(sent, mine_b, mine_b.at[0:31 * PIECE], s_dp))
    pending.append(functools.partial(sent, last_rows, last_rows.at[0:31], s_last, mine_before))
    wait_all(gains.at[0:24], r_pla.at[1])
    store = pltpu.make_async_copy(gains, plane, s_load.at[0])
    store.start()
    wait_all(dpool, r_dp)
    wait_all(spill_back, r_last)
    store.wait()
    for wait in pending:
        wait()


def finish(starts, lengths, dpool, spill_back, inverse_before, out_in, plane, grad, patch_out, gq, gk,
           starts_v, lengths_v, dpool_v, spill_v, inverse_v, out_v, plane_v, grad_v, rows_v, gains_v, s_in, s_to):
    loads = []
    for n, (src, dst) in enumerate(((starts, starts_v), (lengths, lengths_v), (spill_back, spill_v),
                                    (inverse_before, inverse_v), (out_in, out_v), (plane, plane_v))):
        loads.append(pltpu.make_async_copy(src, dst, s_in.at[n]))
    each = HEADS // PARTS
    parts = []
    for p in range(PARTS):
        heads = pl.ds(p * each, each)
        parts.append(pltpu.make_async_copy(dpool.at[heads], dpool_v.at[heads], s_in.at[len(loads) + p]))
    for copy in loads[:4] + parts + loads[4:]:
        copy.start()
    for copy in loads[:4]:
        copy.wait()
    base = lax.axis_index("seq") * 128
    start = starts_v[...] - base
    length = lengths_v[...]
    at_byte = lax.broadcasted_iota(jnp.int32, (128, PIECE), 0)
    inside = (at_byte >= start) & (at_byte < start + length)
    member = inside.astype(f32).astype(bf16)
    by_byte = jnp.sum(jnp.where(inside, 1.0 / length.astype(f32), 0.0), 1, keepdims=True)
    lead = lax.broadcasted_iota(jnp.int32, (8, 1), 0) < start[:, 0:1]
    stores = []

    def store(src, dst):
        stores.append(pltpu.make_async_copy(src, dst, s_to.at[len(stores)]))
        stores[-1].start()

    for p in range(PARTS):
        parts[p].wait()
        for h in range(p * each, (p + 1) * each):
            columns = slice(h * HEAD_DIM, (h + 1) * HEAD_DIM)
            grad_v[:, columns] = jnp.dot(member, dpool_v[h], preferred_element_type=f32) * by_byte
            grad_v[0:8, columns] = jnp.where(lead, spill_v[:, columns] * inverse_v[...], grad_v[0:8, columns])
        columns = pl.ds(p * each * HEAD_DIM, each * HEAD_DIM)
        store(grad_v.at[:, columns], grad.at[:, columns])
    loads[4].wait()
    for h in range(HEADS):
        rows_v[:, h * HEAD_DIM:(h + 1) * HEAD_DIM] = out_v[h]
    store(rows_v, patch_out)
    loads[5].wait()
    for h in range(HEADS):
        for i in range(2):
            gains_v[i, h:h + 1, :] = plane_v[h, i:i + 1, :]
    store(gains_v.at[0], gq)
    store(gains_v.at[1], gk)
    for copy in stores:
        copy.wait()


VMEM = pl.BlockSpec(memory_space=pltpu.VMEM)
ANY = pl.BlockSpec(memory_space=pl.ANY)
DMA = pltpu.SemaphoreType.DMA
PARTS = 4


def shape(dims, dtype):
    return jax.ShapeDtypeStruct(dims, dtype)


def on_device(byte_states, patch_starts, patch_lengths, query_gain, key_gain, out_cotangent):
    states = byte_states[0]
    cot = out_cotangent[0]
    width = states.shape[1]
    own = 2 * BLOCK
    keys = 8 * BLOCK
    by_head = (HEADS, PIECE, HEAD_DIM)
    V = pltpu.VMEM
    out_rows, dpool, spill_back, plane, inverse_before = pl.pallas_call(
        whole,
        out_shape=(shape(by_head, bf16), shape(by_head, bf16), shape((1, width), f32),
                   shape((HEADS, 2, HEAD_DIM), f32), shape((1, HEAD_DIM), f32)),
        in_specs=[ANY, VMEM, VMEM, VMEM, VMEM, ANY],
        out_specs=(ANY,) * 5,
        scratch_shapes=[
            V((128, width), bf16), V((PIECE, width), bf16), V(by_head, bf16), V(by_head, bf16), V((PIECE, width), f32),
            V((1, width), f32), V((1, width), f32), V((1, HEAD_DIM), f32),
            V((128, PIECE, HEAD_DIM), bf16), V((own, HEAD_DIM), bf16), V((own, HEAD_DIM), bf16),
            V((keys, HEAD_DIM), bf16), V((own, HEAD_DIM), bf16),
            V((BLOCK, STEPS * BLOCK), f32), V((BLOCK, STEPS * BLOCK), bf16), V((BLOCK, STEPS * BLOCK), f32),
            V((keys, HEAD_DIM), f32), V((keys, HEAD_DIM), f32),
            V((own, HEAD_DIM), f32), V((2, own, HEAD_DIM), f32), V((2, own, HEAD_DIM), f32), V((own, HEAD_DIM), f32),
            V((own, HEAD_DIM), bf16),
            V((4, BLOCK, HEAD_DIM), f32), V((2, BLOCK, HEAD_DIM), bf16), V((2, BLOCK, HEAD_DIM), bf16),
            V((own, HEAD_DIM), bf16), V((HEADS, 1, HEAD_DIM), f32), V((8, 2, HEAD_DIM), f32),
            V((HEADS, 2, HEAD_DIM), f32),
            DMA((2,)), DMA, DMA, DMA((2,)), DMA((2,)), DMA, DMA, DMA((12,)), DMA((12,)),
            DMA, DMA, DMA((4,)), DMA((4,)), DMA((2,)), DMA((2,)), DMA, DMA, DMA, DMA, DMA((2,)), DMA((2,)),
            DMA, DMA, DMA, DMA,
        ],
        compiler_params=pltpu.CompilerParams(
            collective_id=0, has_side_effects=True, vmem_limit_bytes=56 << 20
        ),
    )(states, patch_starts, patch_lengths, query_gain.reshape(HEADS, HEAD_DIM), key_gain.reshape(HEADS, HEAD_DIM), cot)
    grad, patch_out, gq, gk = pl.pallas_call(
        finish,
        out_shape=(shape((128, width), f32), shape((PIECE, width), bf16),
                   shape((HEADS, HEAD_DIM), f32), shape((HEADS, HEAD_DIM), f32)),
        in_specs=[ANY] * 7,
        out_specs=(ANY,) * 4,
        scratch_shapes=[
            V((1, PIECE), jnp.int32), V((1, PIECE), jnp.int32), V(by_head, bf16), V((1, width), f32),
            V((1, HEAD_DIM), f32), V(by_head, bf16), V((HEADS, 2, HEAD_DIM), f32), V((128, width), f32),
            V((PIECE, width), bf16), V((2, HEADS, HEAD_DIM), f32), DMA((6 + PARTS,)), DMA((3 + PARTS,)),
        ],
        compiler_params=pltpu.CompilerParams(vmem_limit_bytes=62 << 20),
    )(patch_starts, patch_lengths, dpool, spill_back, inverse_before, out_rows, plane)
    return patch_out[None], grad[None], gq.reshape(width), gk.reshape(width)


def solution(mesh):
    rows = P("dp", "seq", None)
    flat = P("dp", "seq")
    return jax.shard_map(
        on_device,
        mesh=mesh,
        in_specs=(rows, flat, flat, P(), P(), rows),
        out_specs=(rows, rows, P(), P()),
        check_vma=False,
    )
```

```python
import functools
import math

import jax
import jax.numpy as jnp
from jax import lax
from jax.experimental import pallas as pl
from jax.experimental.pallas import tpu as pltpu
from jax.sharding import PartitionSpec as P

f32 = jnp.float32
bf16 = jnp.bfloat16
HEAD_DIM = 128
HEADS = 32
PIECE = 32
BLOCK = 512
EPS = 1e-6
NT = (((1,), (1,)), ((), ()))
TN = (((0,), (0,)), ((), ()))


def place():
    seq = lax.axis_index("seq")
    core = lax.axis_index("dp")
    y = seq // 32
    return seq, core, y, (seq // 8) % 4, seq % 8


def at(seq, core):
    return {"seq": seq, "dp": core}


def low_block(y, core):
    return core + 2 * (((y + 1) // 2) % 2)


def owner(y, x, doc):
    block = 2 * y + x // 2
    high = block // 4
    low = block + high * (7 - 2 * block)
    half = low // 2
    return (doc * (3 - half) + (1 - doc) * half), low % 2, high


def source(y, core, i):
    low = low_block(y, core)
    high = i // 16
    block = low + high * (7 - 2 * low)
    return block * 16 + i % 16, y // 2, i * PIECE


def head_at(x, z, i):
    return ((x + i // 8) % 4) * 8 + (z + i % 8) % 8


MESH = pl.DeviceIdType.MESH


def signal(sem, seq, core):
    pl.semaphore_signal(sem, inc=1, device_id=at(seq, core), device_id_type=MESH)


def remote(src, dst, send, recv, seq, core):
    return pltpu.make_async_remote_copy(
        src_ref=src, dst_ref=dst, send_sem=send, recv_sem=recv,
        device_id=at(seq, core), device_id_type=MESH,
    )


def column(row, count):
    r = lax.broadcasted_iota(jnp.int32, (count, count), 0)
    c = lax.broadcasted_iota(jnp.int32, (count, count), 1)
    return jnp.sum(jnp.where(r == c, jnp.broadcast_to(row, (count, count)), 0), 1, keepdims=True)


SCALE = HEAD_DIM ** -0.5
C2 = SCALE * math.log2(math.e)
STEPS = 9
GROUP = BLOCK // HEAD_DIM


def chunk(j):
    return pl.ds(pl.multiple_of(j * BLOCK, BLOCK), BLOCK)


def lanes(x, op):
    parts = [x[:, g * HEAD_DIM:(g + 1) * HEAD_DIM] for g in range(x.shape[1] // HEAD_DIM)]
    return functools.reduce(op, parts)


def step_at(low, doc, t):
    if t in (0, 7, 8):
        return {0: (0, low), 7: (1, low), 8: (1, 7 - low)}[t]
    mask = 3 - (t - 1) // 2
    second = (t - 1) % 2
    chunk_low = (low + mask % 2) % 2 + 2 * ((low // 2 + mask // 2) % 2)
    if t in (5, 6):
        even = 1 - low % 2
        high, mirrored = 1 - second * (1 - even), second * even
    else:
        outer = 1 - low // 2
        high, mirrored = 1 - second * (1 - outer), outer * ((second + doc) % 2)
    return high, chunk_low + mirrored * (7 - 2 * chunk_low)


def group(t):
    return 1 if t in (1, 2, 3, 4) else 0


def tiled(x):
    return jnp.concatenate([x] * GROUP, 1)


def forward(low, doc, values, keyed, query, s_ref, w_ref, stat, delta, mixed, early, sib_keys, far_keys, farsib_keys):
    def cols(t):
        return pl.ds(t * BLOCK, BLOCK)

    stat[...] = jnp.full(stat.shape, -1e30, f32)
    delta[...] = jnp.zeros(delta.shape, f32)
    mixed[...] = jnp.zeros(mixed.shape, f32)

    def scores(steps):
        for t in steps:
            high, j = step_at(low, doc, t)
            s = lax.dot_general(query[chunk(high), :], keyed[chunk(j), :], NT, preferred_element_type=f32)
            if t in (0, 8):
                r = lax.broadcasted_iota(jnp.int32, s.shape, 0)
                c = lax.broadcasted_iota(jnp.int32, s.shape, 1)
                s = jnp.where(c <= r, s, -1e30)
            s_ref[:, cols(t)] = s
            here = stat.at[group(t), chunk(high), :]
            here[...] = jnp.maximum(here[...], lanes(s, jnp.maximum))

    def expo(steps):
        g = group(steps[0])
        stat[g] = jnp.broadcast_to(jnp.max(stat[g], -1, keepdims=True), stat.shape[1:])
        for t in steps:
            high, j = step_at(low, doc, t)
            e = jnp.exp2((s_ref[:, cols(t)] - tiled(stat[g, chunk(high), :])) * C2)
            s_ref[:, cols(t)] = e
            delta[g, chunk(high), :] += lanes(e, jnp.add)

    scores((0, 8, 7))
    early()
    sib_keys()
    scores((5, 6))
    expo((0, 8, 7, 5, 6))
    far_keys()
    scores((3, 4))
    farsib_keys()
    scores((1, 2))
    expo((3, 4, 1, 2))
    top = jnp.maximum(stat[0], stat[1])
    parts = [jnp.exp2((stat[g] - top) * C2) for g in range(2)]
    total = sum(parts[g] * jnp.sum(delta[g], -1, keepdims=True) for g in range(2))
    for g in range(2):
        stat[g] = parts[g] / total

    def mix(steps):
        for t in steps:
            high, j = step_at(low, doc, t)
            w = (s_ref[:, cols(t)] * tiled(stat[group(t), chunk(high), :])).astype(bf16)
            w_ref[:, cols(t)] = w
            mixed[chunk(high), :] += jnp.dot(w, values(j), preferred_element_type=f32)

    for steps in ((0, 8, 7), (5, 6, 3), (4, 1, 2)):
        mix(steps)


def normed(mixed, out):
    m = mixed[...]
    rs = 1.0 / jnp.sqrt(jnp.mean(m * m, -1, keepdims=True) + EPS)
    out[...] = (m * rs).astype(bf16)
    return rs


def backward(low, doc, values, keyed, query, dmb, s_ref, w_ref, d_ref, stat, delta, dk, dv, dq, after):
    def cols(t):
        return pl.ds(t * BLOCK, BLOCK)

    def dvalue(t, high, j):
        dv[chunk(j), :] += lax.dot_general(w_ref[:, cols(t)], dmb[chunk(high), :], TN, preferred_element_type=f32)

    delta[...] = jnp.zeros(delta.shape, f32)

    def dprobs(steps):
        for t in steps:
            high, j = step_at(low, doc, t)
            dp = lax.dot_general(dmb[chunk(high), :], values(j), NT, preferred_element_type=f32)
            d_ref[:, cols(t)] = dp
            delta[group(t), chunk(high), :] += lanes(dp * s_ref[:, cols(t)], jnp.add)

    for steps in ((0, 8, 7), (5, 6, 3), (4, 1, 2)):
        dprobs(steps)
    summed = sum(jnp.sum(delta[g], -1, keepdims=True) * stat[g] for g in range(2))
    delta[0] = summed
    stat[...] = stat[...] * SCALE
    dq[...] = jnp.zeros(dq.shape, f32)

    def dquery(ds, high, j):
        dq[chunk(high), :] += jnp.dot(ds, keyed[chunk(j), :], preferred_element_type=f32)

    def back(steps, far):
        for t in steps:
            high, j = step_at(low, doc, t)
            ds = ((s_ref[:, cols(t)] * tiled(stat[group(t), chunk(high), :]))
                  * (d_ref[:, cols(t)] - tiled(delta[0, chunk(high), :]))).astype(bf16)
            dvalue(t, high, j)
            dk[chunk(j), :] += lax.dot_general(ds, query[chunk(high), :], TN, preferred_element_type=f32)
            if far:
                w_ref[:, cols(t)] = ds
            else:
                dquery(ds, high, j)

    back((1, 3), True)
    after(0)
    back((2, 4), True)
    after(1)
    back((5, 6), False)
    after(2)
    for t in (1, 2, 3, 4):
        dquery(w_ref[:, cols(t)], *step_at(low, doc, t))
    back((0, 8, 7), False)
    after(3)


def whole(states, starts, lengths, qgain_all, kgain_all, cot_rows,
          patch_out, dpool, spill_back, plane, inverse_before,
          bytes_in, cot_in, cot, pooled, sums, spill, spill_in, inverse_out, kfull, cot_h, out_h,
          keyed, query, s_ref, w_ref, d_ref, dk, dv, dq, stat, delta, mixed, dmb,
          from_sib, to_far, from_far, mine_b, last_rows, column_in, gains,
          s_load, s_spill, r_spill, s_pool, r_pool, s_cot, r_cot, s_key, r_key,
          s_out, r_out, s_sib, r_sib, s_far, r_far, s_dp, r_dp, s_col, r_col, s_pla, r_pla,
          s_last, r_last, s_inv, r_inv):
    seq, core, y, x, z = place()
    oy, ocore, ohigh = owner(y, x, core)
    mine = (oy == y) & (ocore == core)
    low = low_block(y, core)
    sib = low + 1 - 2 * (low % 2)
    far = low + 2 - 4 * (low // 2)
    farsib = sib + 2 - 4 * (sib // 2)
    partner = seq + 32 - 64 * (y % 2)
    before = (seq + 127) % 128
    after = (seq + 1) % 128
    head = x * 8 + z
    doc = y // 2
    by, bcore, _high = owner(before // 32, (before // 8) % 4, core)
    mine_before = (by == y) & (bcore == core)
    pending = []

    def wait_all(ref, sem):
        pltpu.make_async_copy(ref, ref, sem).wait()

    def sent(ref, part, sem, own=mine):
        @pl.when(own)
        def _():
            wait_all(part, sem)

        @pl.when(jnp.logical_not(own))
        def _():
            wait_all(ref, sem)

    load_bytes = pltpu.make_async_copy(states, bytes_in, s_load.at[0])
    load_cot = pltpu.make_async_copy(cot_rows, cot_in, s_load.at[1])
    load_bytes.start()
    load_cot.start()

    barrier = pltpu.get_barrier_semaphore()
    signal(barrier, before, core)
    signal(barrier, after, core)

    def greet(i, _):
        s, d, _row = source(y, core, (i + head) % 32)

        @pl.when((s != seq) | (d != core))
        def _():
            signal(barrier, s, d)

        return 0

    lax.fori_loop(0, 32, greet, 0)

    def greet_column(i, _):
        c = (y * 2 + core + i) % 8
        signal(barrier, (c // 2) * 32 + head, c % 2)
        return 0

    lax.fori_loop(1, 8, greet_column, 0)

    base = seq * 128
    start = column(starts[...], PIECE) - base
    length = column(lengths[...], PIECE)
    at_byte = lax.broadcasted_iota(jnp.int32, (PIECE, 128), 1)
    member = ((at_byte >= start) & (at_byte < start + length)).astype(f32).astype(bf16)
    first = starts[:, 0:1] - base
    lead = (lax.broadcasted_iota(jnp.int32, (16, 128), 1) < first).astype(f32).astype(bf16)
    inverse = 1.0 / length.astype(f32)
    inverse_out[...] = jnp.broadcast_to(inverse[PIECE - 1:PIECE, :], (1, HEAD_DIM))
    load_bytes.wait()
    spill[...] = jnp.dot(lead, bytes_in[...], preferred_element_type=f32)[0:1, :]
    sums[...] = jnp.dot(member, bytes_in[...], preferred_element_type=f32) * inverse

    @pl.when(mine)
    def _():
        pl.semaphore_wait(barrier, 31 + 7 + 2)

    @pl.when(jnp.logical_not(mine))
    def _():
        pl.semaphore_wait(barrier, 32 + 7 + 2)

    spilling = remote(spill, spill_in, s_spill, r_spill, before, core)
    spilling.start()
    telling = remote(inverse_out, inverse_before, s_inv, r_inv, after, core)
    telling.start()
    pending.extend([spilling.wait_send, telling.wait])

    def scatter_rows(src, dst, first_row, count, send, recv):
        def step(i, _):
            h = head_at(x, z, i)
            part = src.at[h, pl.ds(first_row, count), :]
            target = oy * 32 + h
            local = (target == seq) & (ocore == core)

            @pl.when(local)
            def _():
                pltpu.make_async_copy(part, dst, recv).start()

            @pl.when(jnp.logical_not(local))
            def _():
                remote(part, dst, send, recv, target, ocore).start()

            return 0

        lax.fori_loop(0, 32, step, 0)

    def by_head(ref, first_row, value):
        for h in range(HEADS):
            ref[h, first_row:first_row + value.shape[0], :] = value[:, h * HEAD_DIM:(h + 1) * HEAD_DIM]

    by_head(pooled, 0, sums[0:16, :].astype(bf16))
    scatter_rows(pooled, kfull.at[seq, pl.ds(0, 16), :], 0, 16, s_pool.at[0], r_pool.at[0])
    spilling.wait_recv()
    last = (lax.broadcasted_iota(jnp.int32, (16, 1), 0) == 15) & (seq < 127)
    by_head(pooled, 16, (sums[16:32, :] + jnp.where(last, spill_in[...] * inverse[16:32, :], 0.0)).astype(bf16))
    scatter_rows(pooled, kfull.at[seq, pl.ds(16, 16), :], 16, 16, s_pool.at[1], r_pool.at[1])
    for i in range(2):
        half = pl.ds(16 * i, 16)
        pending.append(functools.partial(sent, pooled.at[:, half, :], pooled.at[0:31, half, :], s_pool.at[i]))

    qgain = qgain_all[pl.ds(head, 1), :]
    kgain = kgain_all[pl.ds(head, 1), :]

    def clear(j, _):
        dk[chunk(j), :] = jnp.zeros((BLOCK, HEAD_DIM), f32)
        dv[chunk(j), :] = jnp.zeros((BLOCK, HEAD_DIM), f32)
        return 0

    lax.fori_loop(0, 8, clear, 0)
    load_cot.wait()
    by_head(cot, 0, cot_in[...])
    crow = pl.multiple_of(ohigh * BLOCK + (seq % 16) * PIECE, PIECE)

    def pieces(block):
        return pl.ds(block * 16, 16)

    def values(block):
        return kfull[pieces(block)].reshape(BLOCK, HEAD_DIM)

    def prepare(block):
        keyed[chunk(block), :] = (values(block).astype(f32) * kgain).astype(bf16)

    across, beside, relays = {}, {}, {}
    for half in range(2):
        rows = pl.ds(16 * half, 16)
        wait_all(kfull.at[pl.ds(0, 32), rows, :], r_pool.at[half])
        for i, block in enumerate((low, 7 - low)):
            n = 2 * half + i
            there = kfull.at[pieces(block), rows, :]
            across[n] = remote(there, there, s_key.at[n], r_key.at[n], partner, core)
            across[n].start()
            beside[n] = remote(there, there, s_key.at[4 + n], r_key.at[4 + n], seq, 1 - core)
            beside[n].start()
            pending.extend([across[n].wait_send, beside[n].wait_send])
    scatter_rows(cot, cot_h.at[pl.ds(crow, PIECE), :], 0, PIECE, s_cot, r_cot)
    pending.append(functools.partial(sent, cot, cot.at[0:31], s_cot))
    for i, block in enumerate((low, 7 - low)):
        query[chunk(i), :] = (values(block).astype(f32) * qgain).astype(bf16)
        prepare(block)

    def relay(n):
        across[n].wait_recv()
        there = kfull.at[pieces((far, 7 - far)[n % 2]), pl.ds(16 * (n // 2), 16), :]
        relays[n] = remote(there, there, s_key.at[8 + n], r_key.at[8 + n], seq, 1 - core)
        relays[n].start()
        pending.append(relays[n].wait_send)

    def early():
        relay(0)
        relay(1)

    def sib_keys():
        for n in range(4):
            beside[n].wait_recv()
        prepare(sib)
        prepare(7 - sib)

    def far_keys():
        relay(2)
        relay(3)
        prepare(far)
        prepare(7 - far)

    def farsib_keys():
        for n in range(4):
            relays[n].wait_recv()
        prepare(farsib)
        prepare(7 - farsib)

    forward(low, doc, values, keyed, query, s_ref, w_ref, stat, delta, mixed, early, sib_keys, far_keys, farsib_keys)
    rs = normed(mixed, out_h)

    head_columns = pl.ds(pl.multiple_of(head * HEAD_DIM, HEAD_DIM), HEAD_DIM)

    def scatter_back(first, count, part_of, there, send, recv, shift=0):
        def step(i, _):
            n = first + (i + head) % count
            s, d, row = source(y, core, n)
            s = (s + shift) % 128
            part = part_of(n)
            local = (s == seq) & (d == core)

            @pl.when(local)
            def _():
                pltpu.make_async_copy(part, there, recv).start()

            @pl.when(jnp.logical_not(local))
            def _():
                remote(part, there, send, recv, s, d).start()

            return 0

        lax.fori_loop(0, count, step, 0)

    def rows_of(ref):
        return lambda n: ref.at[pl.ds(pl.multiple_of(n * PIECE, PIECE), PIECE), :]

    scatter_back(0, 32, rows_of(out_h), patch_out.at[head], s_out, r_out)
    pending.append(functools.partial(sent, out_h, out_h.at[0:31 * PIECE], s_out))
    pending.append(functools.partial(wait_all, patch_out, r_out))
    wait_all(cot_h, r_cot)
    g = cot_h[...].astype(f32)
    m = mixed[...]
    dmb[...] = (g * rs - m * (jnp.sum(g * m, -1, keepdims=True) * (rs * rs * rs) * (1.0 / HEAD_DIM))).astype(bf16)

    gk = [jnp.zeros((1, HEAD_DIM), f32)]
    to_sib, to_partner = [], []

    def complete(block):
        d = dk[chunk(block), :]
        dv[chunk(block), :] += d * kgain
        gk[0] = gk[0] + jnp.sum(d * values(block).astype(f32), 0, keepdims=True)

    def give_sib(block):
        i = len(to_sib)
        to_sib.append(remote(dv.at[chunk(block), :], from_sib.at[i], s_sib.at[i], r_sib.at[i], seq, 1 - core))
        to_sib[i].start()
        pending.append(to_sib[i].wait_send)

    outer = 1 - low // 2

    def in_turn(block, turn):
        return block + ((turn + 1 + outer * (1 + doc)) % 2) * (7 - 2 * block)

    def combine(turn):
        to_sib[turn].wait_recv()
        to_far[turn] = (dv[chunk(in_turn(far, turn)), :] + from_sib[turn]).astype(bf16)
        to_partner.append(remote(to_far.at[turn], from_far.at[turn], s_far.at[turn], r_far.at[turn], partner, core))
        to_partner[turn].start()
        pending.append(to_partner[turn].wait_send)

    def after_steps(n):
        if n < 2:
            complete(in_turn(farsib, n))
            give_sib(in_turn(farsib, n))
            complete(in_turn(far, n))
        else:
            for block in ((sib, 7 - sib), (low, 7 - low))[n - 2]:
                complete(block)
                if n == 2:
                    give_sib(block)
        if n in (1, 2):
            combine(n - 1)

    backward(low, doc, values, keyed, query, dmb, s_ref, w_ref, d_ref, stat, delta, dk, dv, dq, after_steps)
    gq = jnp.zeros((1, HEAD_DIM), f32)
    for i, block in enumerate((low, 7 - low)):
        gq = gq + jnp.sum(dq[chunk(i), :] * values(block).astype(f32), 0, keepdims=True)
    place_in_column = pl.ds(y * 2 + core, 1)
    column_in[place_in_column] = jnp.concatenate([gq, gk[0]], 0)[None]

    def send_column(i, _):
        c = (y * 2 + core + i) % 8
        slot = column_in.at[place_in_column]
        remote(slot, slot, s_col, r_col, (c // 2) * 32 + head, c % 2).start()
        return 0

    lax.fori_loop(1, 8, send_column, 0)
    to_sib[2].wait_recv()
    to_sib[3].wait_recv()
    for turn in range(2):
        high = (turn + outer + (1 - outer) * doc) % 2
        mixed[chunk(high), :] = (dv[chunk(low + high * (7 - 2 * low)), :] + from_sib[2 + high]
                                 + dq[chunk(high), :] * qgain)
        to_partner[turn].wait_recv()
        mixed[chunk(high), :] += from_far[turn].astype(f32)
        mine_b[chunk(high), :] = mixed[chunk(high), :].astype(bf16)
        scatter_back(16 * high, 16, rows_of(mine_b), dpool.at[head], s_dp, r_dp)
        for i in range(16):
            last_rows[16 * high + i] = mixed[pl.ds(high * BLOCK + i * PIECE + PIECE - 1, 1), :]
        scatter_back(16 * high, 16, lambda n: last_rows.at[n], spill_back.at[:, head_columns], s_last, r_last, 1)
        if turn == 0:
            wait_all(column_in.at[0:7], r_col)
            total = column_in[0]
            for i in range(1, 8):
                total = total + column_in[i]
            gains[pl.ds(head, 1)] = total[None]

            def send_z(i, _):
                slot = gains.at[pl.ds(head, 1)]
                remote(slot, slot, s_pla.at[0], r_pla.at[0], y * 32 + x * 8 + (z + i) % 8, core).start()
                return 0

            lax.fori_loop(1, 8, send_z, 0)
    wait_all(gains.at[0:7], r_pla.at[0])

    def send_x(i, _):
        slots = gains.at[pl.ds(x * 8, 8)]
        remote(slots, slots, s_pla.at[1], r_pla.at[1], y * 32 + ((x + i) % 4) * 8 + z, core).start()
        return 0

    lax.fori_loop(1, 4, send_x, 0)
    pending.append(functools.partial(wait_all, column_in.at[0:7], s_col))
    pending.append(functools.partial(wait_all, gains.at[0:7], s_pla.at[0]))
    pending.append(functools.partial(wait_all, gains.at[0:24], s_pla.at[1]))
    pending.append(functools.partial(sent, mine_b, mine_b.at[0:31 * PIECE], s_dp))
    pending.append(functools.partial(sent, last_rows, last_rows.at[0:31], s_last, mine_before))
    wait_all(gains.at[0:24], r_pla.at[1])
    store = pltpu.make_async_copy(gains, plane, s_load.at[0])
    store.start()
    wait_all(dpool, r_dp)
    wait_all(spill_back, r_last)
    store.wait()
    for wait in pending:
        wait()


def finish(starts, lengths, dpool, spill_back, inverse_before, out_in, plane, grad, patch_out, gq, gk,
           starts_v, lengths_v, dpool_v, spill_v, inverse_v, out_v, plane_v, grad_v, rows_v, gains_v, s_in, s_to):
    loads = []
    for n, (src, dst) in enumerate(((starts, starts_v), (lengths, lengths_v), (spill_back, spill_v),
                                    (inverse_before, inverse_v), (out_in, out_v), (plane, plane_v))):
        loads.append(pltpu.make_async_copy(src, dst, s_in.at[n]))
    each = HEADS // PARTS
    parts = []
    for p in range(PARTS):
        heads = pl.ds(p * each, each)
        parts.append(pltpu.make_async_copy(dpool.at[heads], dpool_v.at[heads], s_in.at[len(loads) + p]))
    for copy in loads[:4] + parts + loads[4:]:
        copy.start()
    for copy in loads[:4]:
        copy.wait()
    base = lax.axis_index("seq") * 128
    start = starts_v[...] - base
    length = lengths_v[...]
    at_byte = lax.broadcasted_iota(jnp.int32, (128, PIECE), 0)
    inside = (at_byte >= start) & (at_byte < start + length)
    member = inside.astype(f32).astype(bf16)
    by_byte = jnp.sum(jnp.where(inside, 1.0 / length.astype(f32), 0.0), 1, keepdims=True)
    lead = lax.broadcasted_iota(jnp.int32, (8, 1), 0) < start[:, 0:1]
    stores = []

    def store(src, dst):
        stores.append(pltpu.make_async_copy(src, dst, s_to.at[len(stores)]))
        stores[-1].start()

    for p in range(PARTS):
        parts[p].wait()
        for h in range(p * each, (p + 1) * each):
            columns = slice(h * HEAD_DIM, (h + 1) * HEAD_DIM)
            grad_v[:, columns] = jnp.dot(member, dpool_v[h], preferred_element_type=f32) * by_byte
            grad_v[0:8, columns] = jnp.where(lead, spill_v[:, columns] * inverse_v[...], grad_v[0:8, columns])
        columns = pl.ds(p * each * HEAD_DIM, each * HEAD_DIM)
        store(grad_v.at[:, columns], grad.at[:, columns])
    loads[4].wait()
    for h in range(HEADS):
        rows_v[:, h * HEAD_DIM:(h + 1) * HEAD_DIM] = out_v[h]
    store(rows_v, patch_out)
    loads[5].wait()
    for h in range(HEADS):
        for i in range(2):
            gains_v[i, h:h + 1, :] = plane_v[h, i:i + 1, :]
    store(gains_v.at[0], gq)
    store(gains_v.at[1], gk)
    for copy in stores:
        copy.wait()


VMEM = pl.BlockSpec(memory_space=pltpu.VMEM)
ANY = pl.BlockSpec(memory_space=pl.ANY)
DMA = pltpu.SemaphoreType.DMA
PARTS = 4


def shape(dims, dtype):
    return jax.ShapeDtypeStruct(dims, dtype)


def on_device(byte_states, patch_starts, patch_lengths, query_gain, key_gain, out_cotangent):
    states = byte_states[0]
    cot = out_cotangent[0]
    width = states.shape[1]
    own = 2 * BLOCK
    keys = 8 * BLOCK
    by_head = (HEADS, PIECE, HEAD_DIM)
    V = pltpu.VMEM
    out_rows, dpool, spill_back, plane, inverse_before = pl.pallas_call(
        whole,
        out_shape=(shape(by_head, bf16), shape(by_head, bf16), shape((1, width), f32),
                   shape((HEADS, 2, HEAD_DIM), f32), shape((1, HEAD_DIM), f32)),
        in_specs=[ANY, VMEM, VMEM, VMEM, VMEM, ANY],
        out_specs=(ANY,) * 5,
        scratch_shapes=[
            V((128, width), bf16), V((PIECE, width), bf16), V(by_head, bf16), V(by_head, bf16), V((PIECE, width), f32),
            V((1, width), f32), V((1, width), f32), V((1, HEAD_DIM), f32),
            V((128, PIECE, HEAD_DIM), bf16), V((own, HEAD_DIM), bf16), V((own, HEAD_DIM), bf16),
            V((keys, HEAD_DIM), bf16), V((own, HEAD_DIM), bf16),
            V((BLOCK, STEPS * BLOCK), f32), V((BLOCK, STEPS * BLOCK), bf16), V((BLOCK, STEPS * BLOCK), f32),
            V((keys, HEAD_DIM), f32), V((keys, HEAD_DIM), f32),
            V((own, HEAD_DIM), f32), V((2, own, HEAD_DIM), f32), V((2, own, HEAD_DIM), f32), V((own, HEAD_DIM), f32),
            V((own, HEAD_DIM), bf16),
            V((4, BLOCK, HEAD_DIM), f32), V((2, BLOCK, HEAD_DIM), bf16), V((2, BLOCK, HEAD_DIM), bf16),
            V((own, HEAD_DIM), bf16), V((HEADS, 1, HEAD_DIM), f32), V((8, 2, HEAD_DIM), f32),
            V((HEADS, 2, HEAD_DIM), f32),
            DMA((2,)), DMA, DMA, DMA((2,)), DMA((2,)), DMA, DMA, DMA((12,)), DMA((12,)),
            DMA, DMA, DMA((4,)), DMA((4,)), DMA((2,)), DMA((2,)), DMA, DMA, DMA, DMA, DMA((2,)), DMA((2,)),
            DMA, DMA, DMA, DMA,
        ],
        compiler_params=pltpu.CompilerParams(
            collective_id=0, has_side_effects=True, vmem_limit_bytes=56 << 20
        ),
    )(states, patch_starts, patch_lengths, query_gain.reshape(HEADS, HEAD_DIM), key_gain.reshape(HEADS, HEAD_DIM), cot)
    grad, patch_out, gq, gk = pl.pallas_call(
        finish,
        out_shape=(shape((128, width), f32), shape((PIECE, width), bf16),
                   shape((HEADS, HEAD_DIM), f32), shape((HEADS, HEAD_DIM), f32)),
        in_specs=[ANY] * 7,
        out_specs=(ANY,) * 4,
        scratch_shapes=[
            V((1, PIECE), jnp.int32), V((1, PIECE), jnp.int32), V(by_head, bf16), V((1, width), f32),
            V((1, HEAD_DIM), f32), V(by_head, bf16), V((HEADS, 2, HEAD_DIM), f32), V((128, width), f32),
            V((PIECE, width), bf16), V((2, HEADS, HEAD_DIM), f32), DMA((6 + PARTS,)), DMA((3 + PARTS,)),
        ],
        compiler_params=pltpu.CompilerParams(vmem_limit_bytes=62 << 20),
    )(patch_starts, patch_lengths, dpool, spill_back, inverse_before, out_rows, plane)
    return patch_out[None], grad[None], gq.reshape(width), gk.reshape(width)


def solution(mesh):
    rows = P("dp", "seq", None)
    flat = P("dp", "seq")
    return jax.shard_map(
        on_device,
        mesh=mesh,
        in_specs=(rows, flat, flat, P(), P(), rows),
        out_specs=(rows, rows, P(), P()),
        check_vma=False,
    )
```
